32 devices in a mesh: groups: 2 (over y), tile: 16 (over z, x, core).
Axes of the slice: x: 2, y: 2, z: 4, core: 2. Of those that a mesh axis runs over, the one named last changes fastest.
Arguments:
- exposure_pixels: bfloat16 [4096, 64, 128], P(('groups', 'tile')), parts along dimension 0, may hold values from -6 to 6
- block_band: int32 [4096], P(('groups', 'tile')), parts along dimension 0, may hold values from 0 to 5
- block_tile: int32 [4096], P(('groups', 'tile')), parts along dimension 0, may hold values from 0 to 15, as said below
- block_row: int32 [4096], P(('groups', 'tile')), parts along dimension 0, may hold values from 0 to 15
- band_weights: bfloat16 [6, 102, 64], replicated, may hold values from -0.75 to 0.75
- psf_kernel: float32 [102, 25], replicated, may hold values from -1 to 1
- gal_tile: int32 [2048], P(('groups', 'tile')), parts along dimension 0, may hold values from 0 to 15, as said below
- gal_row: int32 [2048], P(('groups', 'tile')), parts along dimension 0, may hold values from 0 to 15
- gal_col: int32 [2048], P(('groups', 'tile')), parts along dimension 0, may hold values from 0 to 127
- gal_shift: int32 [2048], P(('groups', 'tile')), parts along dimension 0, may hold values from 0 to 38
Outputs:
- matched_cube: bfloat16 [512, 102, 128], P(('groups', 'tile')), parts along dimension 0
- rest_spectra: bfloat16 [2048, 64], P(('groups', 'tile')), parts along dimension 0
The draws below stay inside these ranges and needn't reach their ends.
There are 2 independent parts, one for each index of `groups`. The reference program is written for one: setup_inputs(seed, part) draws one part's arguments, and reference() takes and returns one part's arrays. A program takes and returns all parts, laid end to end along the dimension named above; an argument that names none is the same for every part. Nothing has to cross between parts.
Inputs may be any that keep to these rules, and one draw needn't show every extreme that they name: `block_tile`: among the 128 blocks of one device at most 16 fall on any one tile; in every draw every device sends exactly 16 blocks to some tile. `gal_tile`: among the 64 catalog entries of one device at most 8 fall on any one tile; in every draw every device has exactly 8 entries on some tile.
All inputs are finite; a program needn't handle non-finite values.
Results may differ from the reference program's by a relative error of at most 0.0054.
Values may be sent and summed in bfloat16 or wider, within the bound.
A program may use at most 128 MiB of HBM per device.

```python
import jax
import jax.numpy as jnp
from jax import lax

C = 102
NBANDS = 6
NS = 64
COLS = 128
KW = 5
NW = 64
TROWS = 16
BLK_DEV = 128
GAL_DEV = 64
CAP = 16
GCAP = 8
BLOCKS = 2048
ROWS = 256
GALAXIES = 1024
N_TILE = 16


def spread_slots(key, capacity, picks):
    key_full, key_favor, key_score, key_order = jax.random.split(key, 4)
    slot_count = N_TILE * capacity
    full_tile = jax.random.randint(key_full, (N_TILE,), 0, N_TILE)
    favor = jax.random.randint(key_favor, (N_TILE,), 0, 4)
    slot_tile = jnp.arange(slot_count, dtype=jnp.int32) // capacity
    score = jax.random.randint(key_score, (N_TILE, slot_count), 0, 1024)
    score = score + 512 * favor[slot_tile][None, :] + 8192 * (slot_tile[None, :] == full_tile[:, None]).astype(jnp.int32)
    score = score * slot_count + jnp.arange(slot_count, dtype=jnp.int32)[None, :]
    chosen = lax.top_k(score, picks)[1]
    order = jax.random.randint(key_order, (N_TILE, picks), 0, 1048576) * picks + jnp.arange(picks, dtype=jnp.int32)[None, :]
    shuffle = jnp.argsort(order, axis=1)
    picked = jnp.take_along_axis(chosen, shuffle, axis=1)
    return (picked // capacity).reshape(-1).astype(jnp.int32)


def draw_block_tile(key, part):
    key = jax.random.fold_in(key, 7)
    return spread_slots(key, CAP, BLK_DEV)


def draw_gal_tile(key, part):
    key = jax.random.fold_in(key, 11)
    return spread_slots(key, GCAP, GAL_DEV)


def plant(array, key, smallest, largest):
    extent = array.shape
    place = [jax.random.randint(jax.random.fold_in(key, axis), (), 0, extent[axis]) for axis in range(len(extent))]
    array = array.at[tuple(place)].set(smallest)
    longest = extent.index(max(extent))
    place[longest] = (place[longest] + 1) % extent[longest]
    return array.at[tuple(place)].set(largest)


def block_levels(rng, extent, cuts, smallest, high):
    def one(position, parts):
        draws = jax.random.uniform(jax.random.fold_in(jax.random.fold_in(rng, 6), position), (parts,), jnp.float32, smallest / len(cuts), high / len(cuts))
        return jnp.repeat(jnp.exp(draws), extent[position] // parts).reshape((-1,) + (1,) * (len(extent) - position - 1))

    factor_of = one(*cuts[0])
    for cut in cuts[1:]:
        factor_of = factor_of * one(*cut)
    return factor_of


def normal_values(stream_key, shape, deviation, reach, pieces=(), kind=jnp.bfloat16):
    entries = jax.random.normal(stream_key, shape, jnp.float32) * deviation
    if len(pieces) > 0:
        entries = block_levels(stream_key, shape, pieces, -0.22, 0.18) * entries
    return jnp.clip(entries, min=-reach, max=reach).astype(kind)


def setup_inputs(seed: int = 0, part: int = 0) -> dict:
    seeds = jax.random.split(jax.random.key(seed), 11)
    part_keys = jax.random.split(jax.random.fold_in(seeds[10], part), 11)
    exposure_pixels = normal_values(part_keys[0], (BLOCKS, NS, COLS), 1.0, 6.0, ((0, 16),))
    block_band = plant(jax.random.randint(part_keys[1], (BLOCKS,), 0, NBANDS), jax.random.fold_in(part_keys[1], 1), 0, NBANDS - 1).astype(jnp.int32)
    block_tile = draw_block_tile(jax.random.fold_in(jax.random.fold_in(seeds[10], part), 71), part)
    block_row = plant(jax.random.randint(part_keys[3], (BLOCKS,), 0, TROWS), jax.random.fold_in(part_keys[3], 1), 0, TROWS - 1).astype(jnp.int32)
    band_weights = normal_values(seeds[4], (NBANDS, C, NS), NS ** -0.5, 0.75)
    psf_kernel = normal_values(seeds[5], (C, KW * KW), 0.2, 1.0, (), jnp.float32)
    gal_tile = draw_gal_tile(jax.random.fold_in(jax.random.fold_in(seeds[10], part), 71), part)
    gal_row = plant(jax.random.randint(part_keys[7], (GALAXIES,), 0, TROWS), jax.random.fold_in(part_keys[7], 1), 0, TROWS - 1).astype(jnp.int32)
    gal_col = plant(jax.random.randint(part_keys[8], (GALAXIES,), 0, COLS), jax.random.fold_in(part_keys[8], 1), 0, COLS - 1).astype(jnp.int32)
    gal_shift = plant(jax.random.randint(part_keys[9], (GALAXIES,), 0, C - NW + 1), jax.random.fold_in(part_keys[9], 1), 0, C - NW).astype(jnp.int32)
    return dict(exposure_pixels=exposure_pixels, block_band=block_band, block_tile=block_tile, block_row=block_row, band_weights=band_weights, psf_kernel=psf_kernel, gal_tile=gal_tile, gal_row=gal_row, gal_col=gal_col, gal_shift=gal_shift)


def reference(exposure_pixels, block_band, block_tile, block_row, band_weights, psf_kernel, gal_tile, gal_row, gal_col, gal_shift):
    weights_wide = band_weights.astype(jnp.float32)
    target = (block_tile * TROWS + block_row).astype(jnp.int32)

    def accumulate(totals, block_step):
        start = (block_step * BLK_DEV).astype(jnp.int32)
        pixels = lax.dynamic_slice_in_dim(exposure_pixels, start, BLK_DEV, 0).astype(jnp.float32)
        bands = lax.dynamic_slice_in_dim(block_band, start, BLK_DEV, 0)
        rows_here = lax.dynamic_slice_in_dim(target, start, BLK_DEV, 0)
        selected = weights_wide[bands]
        spectra = jnp.einsum("bcs,bsp->bcp", selected, pixels).astype(jnp.bfloat16)
        spectra = lax.optimization_barrier(spectra).astype(jnp.float32)
        row_sums = totals[0].at[rows_here].add(spectra)
        counts = totals[1].at[rows_here].add(jnp.ones((BLK_DEV,), jnp.float32))
        return (row_sums, counts), None

    start_sums = jnp.zeros((ROWS, C, COLS), jnp.float32)
    start_counts = jnp.zeros((ROWS,), jnp.float32)
    (row_sums, counts), _ = lax.scan(accumulate, (start_sums, start_counts), jnp.arange(N_TILE, dtype=jnp.int32))
    coadded = (row_sums / jnp.maximum(counts, 1.0)[:, None, None]).astype(jnp.bfloat16)

    radius = KW // 2
    padded = jnp.pad(coadded.astype(jnp.float32), ((radius, radius), (0, 0), (radius, radius)))
    matched_sum = jnp.zeros((ROWS, C, COLS), jnp.float32)
    for offset_row in range(KW):
        for offset_col in range(KW):
            tap_weight = psf_kernel[:, offset_row * KW + offset_col][None, :, None]
            matched_sum = matched_sum + tap_weight * padded[offset_row:offset_row + ROWS, :, offset_col:offset_col + COLS]
    matched_cube = matched_sum.astype(jnp.bfloat16)

    strip_row = (gal_tile * TROWS + gal_row).astype(jnp.int32)
    channel = gal_shift[:, None] + jnp.arange(NW, dtype=jnp.int32)[None, :]
    rest_spectra = matched_cube[strip_row[:, None], channel, gal_col[:, None]]
    return matched_cube, rest_spectra
```

```python
import functools

import jax
import jax.numpy as jnp
from jax import lax
from jax.experimental import pallas as pl
from jax.experimental.pallas import tpu as pltpu
from jax.sharding import PartitionSpec as P

KW = 5
NW = 64
TROWS = 16
F32 = jnp.float32
BF16 = jnp.bfloat16
CHUNKS = 2
GROUP = 8


def partial_sums_kernel(place_ref, band_ref, pixels_ref, weights_ref, *rest):
    outs, total = rest[:-1], rest[-1]
    blocks = pixels_ref.shape[0]
    rows_out = outs[0].shape[0]

    def clear(i, _):
        total[i] = jnp.zeros(total.shape[1:], F32)
        return 0

    lax.fori_loop(0, total.shape[0], clear, 0, unroll=4)

    def step(i, _):
        spectra = []
        for k in range(GROUP):
            b = i * GROUP + k
            spectra.append(
                jnp.dot(weights_ref[band_ref[b]], pixels_ref[b], preferred_element_type=F32)
            )
        for k in range(GROUP):
            b = i * GROUP + k
            total[place_ref[b]] += spectra[k].astype(BF16).astype(F32)
        return 0

    lax.fori_loop(0, blocks // GROUP, step, 0)

    for n, out in enumerate(outs):

        def emit(i, _, n=n, out=out):
            out[i] = total[n * rows_out + i].astype(BF16)
            return 0

        lax.fori_loop(0, rows_out, emit, 0, unroll=4)


def partial_sums(place, band, pixels, weights, rows, pieces):
    channels, columns = weights.shape[1], pixels.shape[2]
    smem = pl.BlockSpec(memory_space=pltpu.SMEM)
    vmem = pl.BlockSpec(memory_space=pltpu.VMEM)
    return pl.pallas_call(
        partial_sums_kernel,
        out_shape=[jax.ShapeDtypeStruct((rows // pieces, channels, columns), BF16)] * pieces,
        in_specs=[smem, smem, vmem, vmem],
        out_specs=[vmem] * pieces,
        scratch_shapes=[pltpu.VMEM((rows, channels, columns), F32)],
        compiler_params=pltpu.CompilerParams(vmem_limit_bytes=48 * 1024 * 1024),
        name="partial_sums",
    )(place, band, pixels, weights)


def tile_row_sums(pixels, band, tile, row, weights):
    me = lax.axis_index("tile")
    z, x, c = me // 4, (me // 2) % 2, me % 2
    dest_z, dest_x, dest_c = tile // 4, (tile // 2) % 2, tile % 2
    far_x, far_c = (dest_x + x) % 2, (dest_c + c) % 2
    part = TROWS // CHUNKS
    place = (((far_c * 2 + far_x) * CHUNKS + row // part) * 4 + dest_z) * part + row % part
    out = partial_sums(place, band, pixels, weights, 16 * TROWS, 4 * CHUNKS)
    other_core = [(i, i ^ 1) for i in range(16)]
    other_x = [(i, i ^ 2) for i in range(16)]
    keep = lambda far, chunk: out[far * CHUNKS + chunk]
    send = lambda far, chunk: out[(2 + far) * CHUNKS + chunk]
    arrived = {}
    for far in (1, 0):
        for chunk in range(CHUNKS):
            arrived[far, chunk] = lax.ppermute(send(far, chunk), "tile", other_core)
    wide = lambda a: a.astype(F32)
    crossed = []
    for chunk in range(CHUNKS):
        chip = (wide(keep(1, chunk)) + wide(arrived[1, chunk])).astype(BF16)
        crossed.append(lax.ppermute(chip, "tile", other_x))
    sums = []
    for chunk in range(CHUNKS):
        plane = (wide(keep(0, chunk)) + wide(arrived[0, chunk]) + wide(crossed[chunk])).astype(BF16)
        plane = plane.reshape((4, part) + plane.shape[1:])
        pick = lambda at: wide(lax.dynamic_index_in_dim(plane, jnp.clip(at, 0, 3), 0, keepdims=False))
        up = down = None
        for dist in (3, 2, 1):
            up_term, down_term = pick(z + dist), pick(z - dist)
            if up is not None:
                up_term, down_term = up_term + wide(up), down_term + wide(down)
            forward = [(i, i + 4) for i in range(4 * (4 - dist))]
            backward = [(15 - i, 15 - j) for i, j in forward]
            up = lax.ppermute(up_term.astype(BF16), "tile", forward)
            down = lax.ppermute(down_term.astype(BF16), "tile", backward)
        sums.append(pick(z) + wide(up) + wide(down))
    return jnp.concatenate(sums, axis=0)


def tile_row_sums_any(pixels, band, tile, row, weights):
    tile_count = lax.axis_size("tile")
    blocks = pixels.shape[0]
    capacity = 2 * blocks // tile_count
    slots = tile_count * capacity
    place = tile * capacity + rank_before(tile)
    tag = jnp.full((slots,), -1, jnp.int32).at[place].set(row * weights.shape[0] + band)
    packed = jnp.zeros((slots,) + pixels.shape[1:], BF16).at[place].set(pixels)
    packed = lax.all_to_all(packed, "tile", split_axis=0, concat_axis=0, tiled=True)
    tag = lax.all_to_all(tag, "tile", split_axis=0, concat_axis=0, tiled=True)
    bands = jnp.maximum(tag, 0) % weights.shape[0]
    rows = jnp.where(tag < 0, -1, tag // weights.shape[0])
    spectra = jnp.einsum("bcs,bsp->bcp", weights[bands], packed, preferred_element_type=F32)
    spectra = spectra.astype(BF16).reshape(slots, -1)
    table = (rows[None, :] == jnp.arange(TROWS)[:, None]).astype(BF16)
    sums = jnp.dot(table, spectra, preferred_element_type=F32)
    return sums.reshape(TROWS, weights.shape[1], pixels.shape[2])


def rank_before(tiles):
    positions = jnp.arange(tiles.shape[0], dtype=jnp.int32)
    earlier = (tiles[:, None] == tiles[None, :]) & (positions[None, :] < positions[:, None])
    return jnp.sum(earlier.astype(jnp.int32), axis=-1)


def with_halo(cells, width):
    count = lax.axis_size("tile")
    ends = count - 1
    above = lax.ppermute(cells[-width:], "tile", [(i, i + 1) for i in range(ends)])
    below = lax.ppermute(cells[:width], "tile", [(i + 1, i) for i in range(ends)])
    return jnp.concatenate([above, cells, below], axis=0)


def psf_match(coadded, psf_kernel):
    radius = KW // 2
    columns = coadded.shape[2]
    padded = jnp.pad(with_halo(coadded, radius), ((0, 0), (0, 0), (radius, radius)))
    total = None
    for dy in range(KW):
        for dx in range(KW):
            tap = psf_kernel[:, dy * KW + dx][None, :, None]
            term = tap * padded[dy : dy + TROWS, :, dx : dx + columns].astype(F32)
            total = term if total is None else total + term
    return total.astype(BF16)


def body(
    exposure_pixels,
    block_band,
    block_tile,
    block_row,
    band_weights,
    psf_kernel,
    gal_tile,
    gal_row,
    gal_col,
    gal_shift,
):
    tile_count = lax.axis_size("tile")
    channels, columns = band_weights.shape[1], exposure_pixels.shape[2]
    gal_here = gal_tile.shape[0]
    depth = min(8, gal_here)
    span = channels - NW + 1
    tile_range = jnp.arange(tile_count, dtype=jnp.int32)
    row_range = jnp.arange(TROWS, dtype=jnp.int32)

    strip_range = jnp.arange(tile_count * TROWS, dtype=jnp.int32)
    target = block_tile * TROWS + block_row
    counts_out = jnp.sum((target[None, :] == strip_range[:, None]).astype(jnp.int32), axis=1)
    place = gal_tile * depth + rank_before(gal_tile)
    word = (gal_row * columns + gal_col) * span + gal_shift
    slot_range = jnp.arange(tile_count * depth, dtype=jnp.int32)
    words_out = jnp.sum(
        jnp.where(place[None, :] == slot_range[:, None], word[None, :], 0), axis=1
    )
    sent = jnp.concatenate(
        [counts_out.reshape(tile_count, TROWS), words_out.reshape(tile_count, depth)], axis=1
    )
    got = lax.all_to_all(sent, "tile", split_axis=0, concat_axis=0, tiled=True)
    counts = jnp.sum(got[:, :TROWS], axis=0).astype(F32)
    words = got[:, TROWS:].reshape(-1)
    slot_shift = words % span
    slot_col = (words // span) % columns
    slot_row = words // (span * columns)

    reduce_rows = tile_row_sums if tile_count == 16 else tile_row_sums_any
    row_sums = reduce_rows(exposure_pixels, block_band, block_tile, block_row, band_weights)
    coadded = (row_sums / jnp.maximum(counts, 1.0)[:, None, None]).astype(BF16)
    matched_cube = psf_match(coadded, psf_kernel)

    column_range = jnp.arange(columns, dtype=jnp.int32)
    chosen = (
        (slot_row[None, None, :] == row_range[:, None, None])
        & (slot_col[None, None, :] == column_range[None, :, None])
    ).astype(BF16)
    spectra = lax.dot_general(
        matched_cube, chosen, (((0, 2), (0, 1)), ((), ())), preferred_element_type=F32
    )
    window = jnp.arange(NW, dtype=jnp.int32)
    channel_range = jnp.arange(channels, dtype=jnp.int32)
    inside = channel_range[None, :, None] == (slot_shift[None, :] + window[:, None])[:, None, :]
    values = jnp.sum(jnp.where(inside, spectra[None], 0.0), axis=1).T.astype(BF16)
    returned = lax.all_to_all(values, "tile", split_axis=0, concat_axis=0, tiled=True)
    mine = (place[:, None] == slot_range[None, :]).astype(BF16)
    rest_spectra = jnp.dot(mine, returned, preferred_element_type=F32).astype(BF16)
    return matched_cube, rest_spectra


def solution(mesh):
    one = P(("groups", "tile"))
    cube = P(("groups", "tile"), None, None)
    return jax.shard_map(
        body,
        mesh=mesh,
        in_specs=(cube, one, one, one, P(), P(), one, one, one, one),
        out_specs=(cube, P(("groups", "tile"), None)),
        check_vma=False,
    )
```

```python
import jax
import jax.numpy as jnp
from jax import lax
from jax.experimental import pallas as pl
from jax.experimental.pallas import tpu as pltpu
from jax.sharding import PartitionSpec as P

KW = 5
NW = 64
TROWS = 16
F32 = jnp.float32
BF16 = jnp.bfloat16
CHUNKS = 4
MESH = pl.DeviceIdType.MESH
GROUP = 8


def partial_sums_kernel(place_ref, band_ref, pixels_ref, weights_ref, keep_ref, send_ref, total):
    blocks = pixels_ref.shape[0]
    half = total.shape[0] // 2

    def clear(i, _):
        total[i] = jnp.zeros(total.shape[1:], F32)
        return 0

    lax.fori_loop(0, total.shape[0], clear, 0, unroll=4)

    def step(i, _):
        spectra = []
        for k in range(GROUP):
            b = i * GROUP + k
            spectra.append(
                jnp.dot(weights_ref[band_ref[b]], pixels_ref[b], preferred_element_type=F32)
            )
        for k in range(GROUP):
            b = i * GROUP + k
            total[place_ref[b]] += spectra[k].astype(BF16).astype(F32)
        return 0

    lax.fori_loop(0, blocks // GROUP, step, 0)

    def emit(i, _):
        keep_ref[i] = total[i].astype(BF16)
        send_ref[i] = total[half + i].astype(BF16)
        return 0

    lax.fori_loop(0, half, emit, 0, unroll=4)


def partial_sums(place, band, pixels, weights, rows):
    channels, columns = weights.shape[1], pixels.shape[2]
    smem = pl.BlockSpec(memory_space=pltpu.SMEM)
    vmem = pl.BlockSpec(memory_space=pltpu.VMEM)
    return pl.pallas_call(
        partial_sums_kernel,
        out_shape=[jax.ShapeDtypeStruct((rows // 2, channels, columns), BF16)] * 2,
        in_specs=[smem, smem, vmem, vmem],
        out_specs=[vmem] * 2,
        scratch_shapes=[pltpu.VMEM((rows, channels, columns), F32)],
        compiler_params=pltpu.CompilerParams(vmem_limit_bytes=40 * 1024 * 1024),
        name="partial_sums",
    )(place, band, pixels, weights)


def greet_all(me, count):
    barrier = pltpu.get_barrier_semaphore()

    def hello(k, _):
        pl.semaphore_signal(
            barrier, inc=1, device_id={"tile": (me + k) % count}, device_id_type=MESH
        )
        return 0

    lax.fori_loop(1, count, hello, 0)
    pl.semaphore_wait(barrier, count - 1)


def exchange_copy(k, me, count, out_ref, in_ref, send_sem, recv_sem):
    there = (me + k) % count
    return pltpu.make_async_remote_copy(
        src_ref=out_ref.at[there],
        dst_ref=in_ref.at[me],
        send_sem=send_sem.at[k],
        recv_sem=recv_sem.at[k],
        device_id={"tile": there},
        device_id_type=MESH,
    )


def reduce_kernel(
    notes_ref, keep_ref, send_ref, rows_ref, notes_out_ref,
    notes_in, from_core, to_x, from_x, plane, chain_out, chain_in, halo_in,
    note_send, note_recv, core_send, core_recv, x_send, x_recv,
    chain_send, chain_recv, halo_send, halo_recv,
):
    count = 16
    me = lax.axis_index("tile")
    z, x, c = me // 4, (me // 2) % 2, me % 2
    other_core = me + 1 - 2 * c
    other_x = me + 2 - 4 * x
    part = TROWS // CHUNKS
    size = 4 * part

    def remote(src, dst, send_sem, recv_sem, there):
        return pltpu.make_async_remote_copy(
            src_ref=src, dst_ref=dst, send_sem=send_sem, recv_sem=recv_sem,
            device_id={"tile": there}, device_id_type=MESH,
        )

    def core_copy(far, k):
        at = far * CHUNKS + k
        rows = pl.ds(at * size, size)
        return remote(
            send_ref.at[rows], from_core.at[rows], core_send.at[at], core_recv.at[at], other_core
        )

    def x_copy(k):
        rows = pl.ds(k * size, size)
        return remote(to_x.at[rows], from_x.at[rows], x_send.at[k], x_recv.at[k], other_x)

    def chain_copy(way, k, dist):
        at = (way * CHUNKS + k) * 3 + dist - 1
        there = (me + 4) % count if way == 0 else (me + 12) % count
        rows = pl.ds(at * part, part)
        return remote(
            chain_out.at[rows], chain_in.at[rows], chain_send.at[at], chain_recv.at[at], there
        )

    def note(k):
        return exchange_copy(k, me, count, notes_ref, notes_in, note_send, note_recv)

    greet_all(me, count)
    for k in range(CHUNKS):
        core_copy(1, k).start()

    def send_note(k, _):
        note(k).start()
        return 0

    lax.fori_loop(1, count, send_note, 0)

    for k in range(CHUNKS):
        core_copy(1, k).wait_recv()

        def add_x(i, _, k=k):
            at = (CHUNKS + k) * size + i
            to_x[k * size + i] = (
                keep_ref[at].astype(F32) + from_core[at].astype(F32)
            ).astype(BF16)
            return 0

        lax.fori_loop(0, size, add_x, 0)
        x_copy(k).start()
    for k in range(CHUNKS):
        core_copy(0, k).start()

    def wait_note(k, total):
        note(k).wait_recv()
        return total

    lax.fori_loop(1, count, wait_note, 0)
    notes_in[me] = notes_ref[me]
    notes_out_ref[...] = notes_in[:, TROWS:, :]
    counts = jnp.maximum(jnp.sum(notes_in[:, :TROWS, :], axis=0).astype(F32), 1.0)

    def sends(way, dist):
        return z + dist <= 3 if way == 0 else z >= dist

    def receives(way, dist):
        if way == 0:
            return jnp.logical_and(z >= 1, z + dist <= 4)
        return jnp.logical_and(z <= 2, z >= dist - 1)

    def hop(k, dist):
        for way in range(2):

            @pl.when(sends(way, dist))
            def _(way=way):
                to_z = z + dist if way == 0 else z - dist
                at = ((way * CHUNKS + k) * 3 + dist - 1) * part
                source = k * size + to_z * part
                edge = z >= 1 if way == 0 else z <= 2
                if dist == 3:
                    def put(i, _):
                        chain_out[at + i] = plane[source + i]
                        return 0

                    lax.fori_loop(0, part, put, 0)
                else:
                    @pl.when(edge)
                    def _():
                        chain_copy(way, k, dist + 1).wait_recv()

                        def put(i, _):
                            chain_out[at + i] = (
                                plane[source + i].astype(F32)
                                + chain_in[at + part + i].astype(F32)
                            ).astype(BF16)
                            return 0

                        lax.fori_loop(0, part, put, 0)

                    @pl.when(jnp.logical_not(edge))
                    def _():
                        def put(i, _):
                            chain_out[at + i] = plane[source + i]
                            return 0

                        lax.fori_loop(0, part, put, 0)
                chain_copy(way, k, dist).start()

    def finish(k):
        up_at, down_at = k * 3 * part, (CHUNKS + k) * 3 * part

        @pl.when(receives(0, 1))
        def _():
            chain_copy(0, k, 1).wait_recv()

        @pl.when(receives(1, 1))
        def _():
            chain_copy(1, k, 1).wait_recv()

        up_on, down_on = z >= 1, z <= 2
        for i in range(part):
            value = plane[k * size + z * part + i].astype(F32)
            value = value + jnp.where(up_on, chain_in[up_at + i].astype(F32), 0.0)
            value = value + jnp.where(down_on, chain_in[down_at + i].astype(F32), 0.0)
            row = k * part + i
            rows_ref[2 + row] = (value / counts[row : row + 1, :]).astype(BF16)

    def halo_copy(way):
        rows = pl.ds(2, 2) if way == 0 else pl.ds(TROWS, 2)
        there = (me + 15) % count if way == 0 else (me + 1) % count
        return remote(
            rows_ref.at[rows], halo_in.at[pl.ds(2 * way, 2)], halo_send.at[way],
            halo_recv.at[way], there,
        )

    def done(k):
        finish(k)
        if k == 0:
            @pl.when(me >= 1)
            def _():
                halo_copy(0).start()
        if k == CHUNKS - 1:
            @pl.when(me <= count - 2)
            def _():
                halo_copy(1).start()

    for k in range(CHUNKS):
        core_copy(0, k).wait_recv()
        x_copy(k).wait_recv()

        def add_plane(i, _, k=k):
            at = k * size + i
            plane[at] = (
                keep_ref[at].astype(F32) + from_core[at].astype(F32) + from_x[at].astype(F32)
            ).astype(BF16)
            return 0

        lax.fori_loop(0, size, add_plane, 0)
        hop(k, 3)
        if k > 0:
            done(k - 1)
        hop(k, 2)
        hop(k, 1)
    done(CHUNKS - 1)

    for i in range(2):
        rows_ref[i] = jnp.zeros(rows_ref.shape[1:], BF16)
        rows_ref[TROWS + 2 + i] = jnp.zeros(rows_ref.shape[1:], BF16)

    @pl.when(me <= count - 2)
    def _():
        halo_copy(0).wait_recv()
        for i in range(2):
            rows_ref[TROWS + 2 + i] = halo_in[i]

    @pl.when(me >= 1)
    def _():
        halo_copy(1).wait_recv()
        for i in range(2):
            rows_ref[i] = halo_in[2 + i]

    @pl.when(me >= 1)
    def _():
        halo_copy(0).wait_send()

    @pl.when(me <= count - 2)
    def _():
        halo_copy(1).wait_send()

    def wait_note_sent(k, _):
        note(k).wait_send()
        return 0

    lax.fori_loop(1, count, wait_note_sent, 0)
    for k in range(CHUNKS):
        core_copy(1, k).wait_send()
        core_copy(0, k).wait_send()
        x_copy(k).wait_send()
        for way in range(2):
            for dist in (3, 2, 1):
                @pl.when(sends(way, dist))
                def _(way=way, k=k, dist=dist):
                    chain_copy(way, k, dist).wait_send()


def reduce_rows_and_notes(notes, keep, send):
    tail = keep.shape[1:]
    vmem = pl.BlockSpec(memory_space=pltpu.VMEM)
    part = TROWS // CHUNKS
    dma = pltpu.SemaphoreType.DMA
    return pl.pallas_call(
        reduce_kernel,
        out_shape=[
            jax.ShapeDtypeStruct((TROWS + 4,) + tail, BF16),
            jax.ShapeDtypeStruct((16, notes.shape[1] - TROWS, 128), jnp.int32),
        ],
        in_specs=[vmem] * 3,
        out_specs=[vmem] * 2,
        scratch_shapes=[
            pltpu.VMEM(notes.shape, jnp.int32),
            pltpu.VMEM((8 * TROWS,) + tail, BF16),
            pltpu.VMEM((4 * TROWS,) + tail, BF16),
            pltpu.VMEM((4 * TROWS,) + tail, BF16),
            pltpu.VMEM((4 * TROWS,) + tail, BF16),
            pltpu.VMEM((6 * TROWS,) + tail, BF16),
            pltpu.VMEM((6 * TROWS,) + tail, BF16),
            pltpu.VMEM((4,) + tail, BF16),
            dma((16,)), dma((16,)),
            dma((2 * CHUNKS,)), dma((2 * CHUNKS,)),
            dma((CHUNKS,)), dma((CHUNKS,)),
            dma((6 * CHUNKS,)), dma((6 * CHUNKS,)),
            dma((2,)), dma((2,)),
        ],
        compiler_params=pltpu.CompilerParams(
            collective_id=0, has_side_effects=True, vmem_limit_bytes=40 * 1024 * 1024
        ),
        name="reduce_rows",
    )(notes, keep, send)


def exchange_kernel(out_ref, in_ref, landed, send_sem, recv_sem):
    count = out_ref.shape[0]
    me = lax.axis_index("tile")

    def copy(k):
        return exchange_copy(k, me, count, out_ref, landed, send_sem, recv_sem)

    greet_all(me, count)

    def start(k, _):
        copy(k).start()
        return 0

    def wait(k, _):
        copy(k).wait()
        return 0

    lax.fori_loop(1, count, start, 0)
    landed[me] = out_ref[me]
    lax.fori_loop(1, count, wait, 0)
    in_ref[...] = landed[...]


def exchange(values):
    vmem = pl.BlockSpec(memory_space=pltpu.VMEM)
    return pl.pallas_call(
        exchange_kernel,
        out_shape=jax.ShapeDtypeStruct(values.shape, values.dtype),
        in_specs=[vmem],
        out_specs=vmem,
        scratch_shapes=[
            pltpu.VMEM(values.shape, values.dtype),
            pltpu.SemaphoreType.DMA((values.shape[0],)),
            pltpu.SemaphoreType.DMA((values.shape[0],)),
        ],
        compiler_params=pltpu.CompilerParams(
            collective_id=1, has_side_effects=True, vmem_limit_bytes=40 * 1024 * 1024
        ),
        name="exchange",
    )(values)


def averaged_rows(pixels, band, tile, row, weights, counts_out, words_out):
    me = lax.axis_index("tile")
    x, c = (me // 2) % 2, me % 2
    dest_z, dest_x, dest_c = tile // 4, (tile // 2) % 2, tile % 2
    far_x, far_c = (dest_x + x) % 2, (dest_c + c) % 2
    part = TROWS // CHUNKS
    place = (((far_c * 2 + far_x) * CHUNKS + row // part) * 4 + dest_z) * part + row % part
    keep, send = partial_sums(place, band, pixels, weights, 16 * TROWS)
    notes = jnp.concatenate([counts_out, words_out], axis=1)
    notes = jnp.broadcast_to(notes[:, :, None], notes.shape + (128,))
    rows, notes = reduce_rows_and_notes(notes, keep, send)
    return rows, notes[:, :, 0].reshape(-1)


def averaged_rows_any(pixels, band, tile, row, weights, counts_out, words_out):
    sent = jnp.concatenate([counts_out, words_out], axis=1)
    got = lax.all_to_all(sent, "tile", split_axis=0, concat_axis=0, tiled=True)
    counts = jnp.sum(got[:, :TROWS], axis=0).astype(F32)
    row_sums = tile_row_sums_any(pixels, band, tile, row, weights)
    rows = (row_sums / jnp.maximum(counts, 1.0)[:, None, None]).astype(BF16)
    return with_halo(rows, KW // 2), got[:, TROWS:].reshape(-1)


def tile_row_sums_any(pixels, band, tile, row, weights):
    tile_count = lax.axis_size("tile")
    blocks = pixels.shape[0]
    capacity = 2 * blocks // tile_count
    slots = tile_count * capacity
    place = tile * capacity + rank_before(tile)
    tag = jnp.full((slots,), -1, jnp.int32).at[place].set(row * weights.shape[0] + band)
    packed = jnp.zeros((slots,) + pixels.shape[1:], BF16).at[place].set(pixels)
    packed = lax.all_to_all(packed, "tile", split_axis=0, concat_axis=0, tiled=True)
    tag = lax.all_to_all(tag, "tile", split_axis=0, concat_axis=0, tiled=True)
    bands = jnp.maximum(tag, 0) % weights.shape[0]
    rows = jnp.where(tag < 0, -1, tag // weights.shape[0])
    spectra = jnp.einsum("bcs,bsp->bcp", weights[bands], packed, preferred_element_type=F32)
    spectra = spectra.astype(BF16).reshape(slots, -1)
    table = (rows[None, :] == jnp.arange(TROWS)[:, None]).astype(BF16)
    sums = jnp.dot(table, spectra, preferred_element_type=F32)
    return sums.reshape(TROWS, weights.shape[1], pixels.shape[2])


def rank_before(tiles):
    positions = jnp.arange(tiles.shape[0], dtype=jnp.int32)
    earlier = (tiles[:, None] == tiles[None, :]) & (positions[None, :] < positions[:, None])
    return jnp.sum(earlier.astype(jnp.int32), axis=-1)


def with_halo(cells, width):
    count = lax.axis_size("tile")
    ends = count - 1
    above = lax.ppermute(cells[-width:], "tile", [(i, i + 1) for i in range(ends)])
    below = lax.ppermute(cells[:width], "tile", [(i + 1, i) for i in range(ends)])
    return jnp.concatenate([above, cells, below], axis=0)


def psf_match(coadded, psf_kernel):
    radius = KW // 2
    columns = coadded.shape[2]
    padded = jnp.pad(coadded, ((0, 0), (0, 0), (radius, radius)))
    total = None
    for dy in range(KW):
        for dx in range(KW):
            tap = psf_kernel[:, dy * KW + dx][None, :, None]
            term = tap * padded[dy : dy + TROWS, :, dx : dx + columns].astype(F32)
            total = term if total is None else total + term
    return total.astype(BF16)


def body(
    exposure_pixels,
    block_band,
    block_tile,
    block_row,
    band_weights,
    psf_kernel,
    gal_tile,
    gal_row,
    gal_col,
    gal_shift,
):
    tile_count = lax.axis_size("tile")
    channels, columns = band_weights.shape[1], exposure_pixels.shape[2]
    gal_here = gal_tile.shape[0]
    depth = min(8, gal_here)
    span = channels - NW + 1
    tile_range = jnp.arange(tile_count, dtype=jnp.int32)
    row_range = jnp.arange(TROWS, dtype=jnp.int32)

    strip_range = jnp.arange(tile_count * TROWS, dtype=jnp.int32)
    target = block_tile * TROWS + block_row
    counts_out = jnp.sum((target[None, :] == strip_range[:, None]).astype(jnp.int32), axis=1)
    place = gal_tile * depth + rank_before(gal_tile)
    word = (gal_row * columns + gal_col) * span + gal_shift
    slot_range = jnp.arange(tile_count * depth, dtype=jnp.int32)
    words_out = jnp.sum(
        jnp.where(place[None, :] == slot_range[:, None], word[None, :], 0), axis=1
    )
    small = tile_count == 16
    coadded, words = (averaged_rows if small else averaged_rows_any)(
        exposure_pixels, block_band, block_tile, block_row, band_weights,
        counts_out.reshape(tile_count, TROWS), words_out.reshape(tile_count, depth),
    )
    slot_shift = words % span
    slot_col = (words // span) % columns
    slot_row = words // (span * columns)
    matched_cube = psf_match(coadded, psf_kernel)

    column_range = jnp.arange(columns, dtype=jnp.int32)
    chosen = (
        (slot_row[None, None, :] == row_range[:, None, None])
        & (slot_col[None, None, :] == column_range[None, :, None])
    ).astype(BF16)
    spectra = lax.dot_general(
        matched_cube, chosen, (((0, 2), (0, 1)), ((), ())), preferred_element_type=F32
    )
    window = jnp.arange(NW, dtype=jnp.int32)
    channel_range = jnp.arange(channels, dtype=jnp.int32)
    inside = channel_range[None, :, None] == (slot_shift[None, :] + window[:, None])[:, None, :]
    values = jnp.sum(jnp.where(inside, spectra[None], 0.0), axis=1).T.astype(BF16)
    if small:
        values = jnp.pad(values, ((0, 0), (0, 128 - NW))).astype(F32)
        returned = exchange(values.reshape(tile_count, depth, 128))
        returned = returned.reshape(-1, 128)[:, :NW].astype(BF16)
    else:
        returned = lax.all_to_all(values, "tile", split_axis=0, concat_axis=0, tiled=True)
    mine = (place[:, None] == slot_range[None, :]).astype(BF16)
    rest_spectra = jnp.dot(mine, returned, preferred_element_type=F32).astype(BF16)
    return matched_cube, rest_spectra


def solution(mesh):
    one = P(("groups", "tile"))
    cube = P(("groups", "tile"), None, None)
    return jax.shard_map(
        body,
        mesh=mesh,
        in_specs=(cube, one, one, one, P(), P(), one, one, one, one),
        out_specs=(cube, P(("groups", "tile"), None)),
        check_vma=False,
    )
```

```python
import jax
import jax.numpy as jnp
from jax import lax
from jax.experimental import pallas as pl
from jax.experimental.pallas import tpu as pltpu
from jax.sharding import PartitionSpec as P

KW = 5
NW = 64
TROWS = 16
F32 = jnp.float32
BF16 = jnp.bfloat16
CHUNKS = 8
PART = TROWS // CHUNKS
SLAB = 4 * PART
ORDER = (0, 7, 1, 2, 3, 4, 5, 6)
MESH = pl.DeviceIdType.MESH
GROUP = 8


def partial_sums_kernel(
    place_ref, band_ref, pixels_ref, weights_ref, keep_hbm, send_hbm,
    total, keep_ref, send_ref, out_sem,
):
    blocks = pixels_ref.shape[0]
    half = total.shape[0] // 2

    def clear(i, _):
        total[i] = jnp.zeros(total.shape[1:], F32)
        return 0

    lax.fori_loop(0, total.shape[0], clear, 0, unroll=4)

    def step(i, _):
        spectra = []
        for k in range(GROUP):
            b = i * GROUP + k
            spectra.append(
                jnp.dot(weights_ref[band_ref[b]], pixels_ref[b], preferred_element_type=F32)
            )
        for k in range(GROUP):
            b = i * GROUP + k
            total[place_ref[b]] += spectra[k].astype(BF16).astype(F32)
        return 0

    lax.fori_loop(0, blocks // GROUP, step, 0)

    copies = []
    for far in (1, 0):
        rows = pl.ds(far * half // 2, half // 2)
        for n, (buffer, out) in enumerate(((send_ref, send_hbm), (keep_ref, keep_hbm))):
            source = (half if n == 0 else 0) + far * half // 2

            def emit(i, _, buffer=buffer, source=source, far=far):
                buffer[far * half // 2 + i] = total[source + i].astype(BF16)
                return 0

            lax.fori_loop(0, half // 2, emit, 0, unroll=4)
            copy = pltpu.make_async_copy(buffer.at[rows], out.at[rows], out_sem.at[2 * far + n])
            copy.start()
            copies.append(copy)
    for copy in copies:
        copy.wait()


def partial_sums(place, band, pixels, weights, rows):
    channels, columns = weights.shape[1], pixels.shape[2]
    smem = pl.BlockSpec(memory_space=pltpu.SMEM)
    vmem = pl.BlockSpec(memory_space=pltpu.VMEM)
    return pl.pallas_call(
        partial_sums_kernel,
        out_shape=[jax.ShapeDtypeStruct((rows // 2, channels, columns), BF16)] * 2,
        in_specs=[smem, smem, vmem, vmem],
        out_specs=[pl.BlockSpec(memory_space=pltpu.HBM)] * 2,
        scratch_shapes=[
            pltpu.VMEM((rows, channels, columns), F32),
            pltpu.VMEM((rows // 2, channels, columns), BF16),
            pltpu.VMEM((rows // 2, channels, columns), BF16),
            pltpu.SemaphoreType.DMA((4,)),
        ],
        compiler_params=pltpu.CompilerParams(vmem_limit_bytes=40 * 1024 * 1024),
        name="partial_sums",
    )(place, band, pixels, weights)


def greet_all(me, count):
    barrier = pltpu.get_barrier_semaphore()

    def hello(k, _):
        pl.semaphore_signal(
            barrier, inc=1, device_id={"tile": (me + k) % count}, device_id_type=MESH
        )
        return 0

    lax.fori_loop(1, count, hello, 0)
    pl.semaphore_wait(barrier, count - 1)


def exchange_copy(k, me, count, out_ref, in_ref, send_sem, recv_sem):
    there = (me + k) % count
    return pltpu.make_async_remote_copy(
        src_ref=out_ref.at[there],
        dst_ref=in_ref.at[me],
        send_sem=send_sem.at[k],
        recv_sem=recv_sem.at[k],
        device_id={"tile": there},
        device_id_type=MESH,
    )


def reduce_kernel(
    notes_ref, keep_hbm, send_ref, psf_ref, mine_ref, cube_ref, rest_ref,
    notes_in, keep_ref, from_core, to_x, from_x, plane, chain_out, chain_in, halo_in, rows_ref,
    taps, picked, window_out, window_in,
    note_send, note_recv, window_send, window_recv, keep_sem, core_send, core_recv, x_send, x_recv,
    chain_send, chain_recv, halo_send, halo_recv,
):
    count = 16
    me = lax.axis_index("tile")
    z, x, c = me // 4, (me // 2) % 2, me % 2
    other_core = me + 1 - 2 * c
    other_x = me + 2 - 4 * x
    part, size = PART, SLAB
    channels, columns = cube_ref.shape[1], cube_ref.shape[2]

    def remote(src, dst, send_sem, recv_sem, there):
        return pltpu.make_async_remote_copy(
            src_ref=src, dst_ref=dst, send_sem=send_sem, recv_sem=recv_sem,
            device_id={"tile": there}, device_id_type=MESH,
        )

    def core_copy(far, k):
        at = far * CHUNKS + k
        rows = pl.ds(at * size, size)
        return remote(
            send_ref.at[rows], from_core.at[rows], core_send.at[at], core_recv.at[at], other_core
        )

    def x_copy(k):
        rows = pl.ds(k * size, size)
        return remote(to_x.at[rows], from_x.at[rows], x_send.at[k], x_recv.at[k], other_x)

    def chain_copy(way, k, dist):
        at = (way * CHUNKS + k) * 3 + dist - 1
        there = (me + 4) % count if way == 0 else (me + 12) % count
        rows = pl.ds(at * part, part)
        return remote(
            chain_out.at[rows], chain_in.at[rows], chain_send.at[at], chain_recv.at[at], there
        )

    def note(k):
        return exchange_copy(k, me, count, notes_ref, notes_in, note_send, note_recv)

    def window(k):
        return exchange_copy(k, me, count, window_out, window_in, window_send, window_recv)

    def keep_copy(far):
        rows = pl.ds(far * CHUNKS * size, CHUNKS * size)
        return pltpu.make_async_copy(keep_hbm.at[rows], keep_ref.at[rows], keep_sem.at[far])

    keep_copy(1).start()
    keep_copy(0).start()
    greet_all(me, count)
    for k in range(CHUNKS):
        core_copy(1, k).start()

    def send_note(k, _):
        note(k).start()
        return 0

    lax.fori_loop(1, count, send_note, 0)

    keep_copy(1).wait()
    for k in range(CHUNKS):
        core_copy(1, k).wait_recv()

        def add_x(i, _, k=k):
            at = (CHUNKS + k) * size + i
            to_x[k * size + i] = (
                keep_ref[at].astype(F32) + from_core[at].astype(F32)
            ).astype(BF16)
            return 0

        lax.fori_loop(0, size, add_x, 0)
        x_copy(k).start()
    for k in range(CHUNKS):
        core_copy(0, k).start()

    def wait_note(k, total):
        note(k).wait_recv()
        return total

    lax.fori_loop(1, count, wait_note, 0)
    notes_in[me] = notes_ref[me]
    keep_copy(0).wait()
    words = notes_in[:, TROWS:, :].reshape(-1, 128)
    slot_shift = words & 63
    slot_col = (words >> 6) & 127
    slot_row = words >> 13
    lane = lax.broadcasted_iota(jnp.int32, words.shape, 1)
    on_column = slot_col == lane
    picked[...] = jnp.zeros(picked.shape, F32)
    for tap in range(KW * KW):
        taps[tap] = jnp.broadcast_to(psf_ref[:, tap : tap + 1], (channels, columns))
    counts = jnp.maximum(jnp.sum(notes_in[:, :TROWS, :], axis=0).astype(F32), 1.0)

    def sends(way, dist):
        return z + dist <= 3 if way == 0 else z >= dist

    def receives(way, dist):
        if way == 0:
            return jnp.logical_and(z >= 1, z + dist <= 4)
        return jnp.logical_and(z <= 2, z >= dist - 1)

    def hop(k, dist):
        for way in range(2):

            @pl.when(sends(way, dist))
            def _(way=way):
                to_z = z + dist if way == 0 else z - dist
                at = ((way * CHUNKS + k) * 3 + dist - 1) * part
                source = k * size + to_z * part
                edge = z >= 1 if way == 0 else z <= 2
                if dist == 3:
                    def put(i, _):
                        chain_out[at + i] = plane[source + i]
                        return 0

                    lax.fori_loop(0, part, put, 0)
                else:
                    @pl.when(edge)
                    def _():
                        chain_copy(way, k, dist + 1).wait_recv()

                        def put(i, _):
                            chain_out[at + i] = (
                                plane[source + i].astype(F32)
                                + chain_in[at + part + i].astype(F32)
                            ).astype(BF16)
                            return 0

                        lax.fori_loop(0, part, put, 0)

                    @pl.when(jnp.logical_not(edge))
                    def _():
                        def put(i, _):
                            chain_out[at + i] = plane[source + i]
                            return 0

                        lax.fori_loop(0, part, put, 0)
                chain_copy(way, k, dist).start()

    def finish(k):
        up_at, down_at = k * 3 * part, (CHUNKS + k) * 3 * part

        @pl.when(receives(0, 1))
        def _():
            chain_copy(0, k, 1).wait_recv()

        @pl.when(receives(1, 1))
        def _():
            chain_copy(1, k, 1).wait_recv()

        up_on, down_on = z >= 1, z <= 2
        for i in range(part):
            value = plane[k * size + z * part + i].astype(F32)
            value = value + jnp.where(up_on, chain_in[up_at + i].astype(F32), 0.0)
            value = value + jnp.where(down_on, chain_in[down_at + i].astype(F32), 0.0)
            row = ORDER[k] * part + i
            rows_ref[2 + row] = (value / counts[row : row + 1, :]).astype(BF16)

    def halo_copy(way):
        rows = pl.ds(2, 2) if way == 0 else pl.ds(TROWS, 2)
        there = (me + 15) % count if way == 0 else (me + 1) % count
        return remote(
            rows_ref.at[rows], halo_in.at[pl.ds(2 * way, 2)], halo_send.at[way],
            halo_recv.at[way], there,
        )

    def match_row(y, _):
        radius = KW // 2
        near = [rows_ref[y + dy].astype(F32) for dy in range(KW)]
        at = lax.broadcasted_iota(jnp.int32, (channels, columns), 1)
        total = None
        for dx in range(KW):
            term = taps[dx] * near[0]
            for dy in range(1, KW):
                term = term + taps[dy * KW + dx] * near[dy]
            offset = dx - radius
            if offset != 0:
                term = pltpu.roll(term, (-offset) % columns, 1)
                valid = at < columns - offset if offset > 0 else at >= -offset
                term = jnp.where(valid, term, 0.0)
            total = term if total is None else total + term
        matched = total.astype(BF16)
        cube_ref[y] = matched
        chosen = jnp.where(jnp.logical_and(on_column, slot_row == y), 1.0, 0.0).astype(BF16)
        picked[:, :channels] += lax.dot_general(
            chosen, matched, (((1,), (1,)), ((), ())), preferred_element_type=F32
        )
        return 0

    def take_halo():
        @pl.when(me <= count - 2)
        def _():
            halo_copy(0).wait_recv()
            for i in range(2):
                rows_ref[TROWS + 2 + i] = halo_in[i]

        @pl.when(me >= 1)
        def _():
            halo_copy(1).wait_recv()
            for i in range(2):
                rows_ref[i] = halo_in[2 + i]

    def done(k):
        finish(k)
        if k == 0:
            @pl.when(me >= 1)
            def _():
                halo_copy(0).start()
        if k == 1:
            @pl.when(me <= count - 2)
            def _():
                halo_copy(1).start()
        if k == 4:
            take_halo()
            lax.fori_loop(0, 2, match_row, 0)
        if k >= 3:
            lax.fori_loop(2 * k - 4, 2 * k - 2 if k < CHUNKS - 1 else TROWS, match_row, 0)

    for i in range(2):
        rows_ref[i] = jnp.zeros(rows_ref.shape[1:], BF16)
        rows_ref[TROWS + 2 + i] = jnp.zeros(rows_ref.shape[1:], BF16)

    for t in range(CHUNKS + 3):
        if t < CHUNKS:
            core_copy(0, t).wait_recv()
            x_copy(t).wait_recv()

            def add_plane(i, _, t=t):
                at = t * size + i
                plane[at] = (
                    keep_ref[at].astype(F32) + from_core[at].astype(F32) + from_x[at].astype(F32)
                ).astype(BF16)
                return 0

            lax.fori_loop(0, size, add_plane, 0)
            hop(t, 3)
        if 0 <= t - 1 < CHUNKS:
            hop(t - 1, 2)
        if 0 <= t - 2 < CHUNKS:
            hop(t - 2, 1)
        if t >= 3:
            done(t - 3)

    chosen_window = picked[...]
    for bit in range(6):
        moved = pltpu.roll(chosen_window, 128 - 2**bit, 1)
        chosen_window = jnp.where((slot_shift >> bit) & 1 == 1, moved, chosen_window)
    window_out[...] = chosen_window.reshape(window_out.shape)

    def send_window(k, _):
        window(k).start()
        return 0

    def take_window(k, _):
        window(k).wait()
        return 0

    lax.fori_loop(1, count, send_window, 0)
    window_in[me] = window_out[me]

    @pl.when(me >= 1)
    def _():
        halo_copy(0).wait_send()

    @pl.when(me <= count - 2)
    def _():
        halo_copy(1).wait_send()

    def wait_note_sent(k, _):
        note(k).wait_send()
        return 0

    lax.fori_loop(1, count, wait_note_sent, 0)
    for k in range(CHUNKS):
        core_copy(1, k).wait_send()
        core_copy(0, k).wait_send()
        x_copy(k).wait_send()
        for way in range(2):
            for dist in (3, 2, 1):
                @pl.when(sends(way, dist))
                def _(way=way, k=k, dist=dist):
                    chain_copy(way, k, dist).wait_send()
    lax.fori_loop(1, count, take_window, 0)
    landed = window_in[...].reshape(-1, 128).astype(BF16)
    rest = jnp.dot(mine_ref[...], landed, preferred_element_type=F32)
    rest_ref[...] = rest[:, :NW].astype(BF16)


def reduce_and_match(notes, keep, send, psf_kernel, mine):
    tail = keep.shape[1:]
    vmem = pl.BlockSpec(memory_space=pltpu.VMEM)
    hbm = pl.BlockSpec(memory_space=pltpu.HBM)
    dma = pltpu.SemaphoreType.DMA
    slots = mine.shape[1]
    return pl.pallas_call(
        reduce_kernel,
        out_shape=[
            jax.ShapeDtypeStruct((TROWS,) + tail, BF16),
            jax.ShapeDtypeStruct((mine.shape[0], NW), BF16),
        ],
        in_specs=[vmem, hbm, hbm, vmem, vmem],
        out_specs=[vmem] * 2,
        scratch_shapes=[
            pltpu.VMEM(notes.shape, jnp.int32),
            pltpu.VMEM((8 * TROWS,) + tail, BF16),
            pltpu.VMEM((8 * TROWS,) + tail, BF16),
            pltpu.VMEM((4 * TROWS,) + tail, BF16),
            pltpu.VMEM((4 * TROWS,) + tail, BF16),
            pltpu.VMEM((4 * TROWS,) + tail, BF16),
            pltpu.VMEM((6 * TROWS,) + tail, BF16),
            pltpu.VMEM((6 * TROWS,) + tail, BF16),
            pltpu.VMEM((4,) + tail, BF16),
            pltpu.VMEM((TROWS + 4,) + tail, BF16),
            pltpu.VMEM((KW * KW,) + tail, F32),
            pltpu.VMEM((slots, 128), F32),
            pltpu.VMEM((16, slots // 16, 128), F32),
            pltpu.VMEM((16, slots // 16, 128), F32),
            dma((16,)), dma((16,)), dma((16,)), dma((16,)), dma((2,)),
            dma((2 * CHUNKS,)), dma((2 * CHUNKS,)),
            dma((CHUNKS,)), dma((CHUNKS,)),
            dma((6 * CHUNKS,)), dma((6 * CHUNKS,)),
            dma((2,)), dma((2,)),
        ],
        compiler_params=pltpu.CompilerParams(
            collective_id=0, has_side_effects=True, vmem_limit_bytes=48 * 1024 * 1024
        ),
        name="reduce_and_match",
    )(notes, keep, send, psf_kernel, mine)


def small_body(pixels, band, tile, row, weights, psf_kernel, counts_out, words_out, mine):
    me = lax.axis_index("tile")
    x, c = (me // 2) % 2, me % 2
    dest_z, dest_x, dest_c = tile // 4, (tile // 2) % 2, tile % 2
    far_x, far_c = (dest_x + x) % 2, (dest_c + c) % 2
    pair = row // PART
    chunk = jnp.where(pair == 0, 0, jnp.where(pair == CHUNKS - 1, 1, pair + 1))
    place = (((far_c * 2 + far_x) * CHUNKS + chunk) * 4 + dest_z) * PART + row % PART
    keep, send = partial_sums(place, band, pixels, weights, 16 * TROWS)
    notes = jnp.concatenate([counts_out, words_out], axis=1)
    notes = jnp.broadcast_to(notes[:, :, None], notes.shape + (128,))
    return reduce_and_match(notes, keep, send, psf_kernel, mine)


def averaged_rows_any(pixels, band, tile, row, weights, counts_out, words_out):
    sent = jnp.concatenate([counts_out, words_out], axis=1)
    got = lax.all_to_all(sent, "tile", split_axis=0, concat_axis=0, tiled=True)
    counts = jnp.sum(got[:, :TROWS], axis=0).astype(F32)
    row_sums = tile_row_sums_any(pixels, band, tile, row, weights)
    rows = (row_sums / jnp.maximum(counts, 1.0)[:, None, None]).astype(BF16)
    return with_halo(rows, KW // 2), got[:, TROWS:].reshape(-1)


def tile_row_sums_any(pixels, band, tile, row, weights):
    tile_count = lax.axis_size("tile")
    blocks = pixels.shape[0]
    capacity = 2 * blocks // tile_count
    slots = tile_count * capacity
    place = tile * capacity + rank_before(tile)
    tag = jnp.full((slots,), -1, jnp.int32).at[place].set(row * weights.shape[0] + band)
    packed = jnp.zeros((slots,) + pixels.shape[1:], BF16).at[place].set(pixels)
    packed = lax.all_to_all(packed, "tile", split_axis=0, concat_axis=0, tiled=True)
    tag = lax.all_to_all(tag, "tile", split_axis=0, concat_axis=0, tiled=True)
    bands = jnp.maximum(tag, 0) % weights.shape[0]
    rows = jnp.where(tag < 0, -1, tag // weights.shape[0])
    spectra = jnp.einsum("bcs,bsp->bcp", weights[bands], packed, preferred_element_type=F32)
    spectra = spectra.astype(BF16).reshape(slots, -1)
    table = (rows[None, :] == jnp.arange(TROWS)[:, None]).astype(BF16)
    sums = jnp.dot(table, spectra, preferred_element_type=F32)
    return sums.reshape(TROWS, weights.shape[1], pixels.shape[2])


def rank_before(tiles):
    positions = jnp.arange(tiles.shape[0], dtype=jnp.int32)
    earlier = (tiles[:, None] == tiles[None, :]) & (positions[None, :] < positions[:, None])
    return jnp.sum(earlier.astype(jnp.int32), axis=-1)


def with_halo(cells, width):
    count = lax.axis_size("tile")
    ends = count - 1
    above = lax.ppermute(cells[-width:], "tile", [(i, i + 1) for i in range(ends)])
    below = lax.ppermute(cells[:width], "tile", [(i + 1, i) for i in range(ends)])
    return jnp.concatenate([above, cells, below], axis=0)


def psf_match(coadded, psf_kernel):
    radius = KW // 2
    columns = coadded.shape[2]
    padded = jnp.pad(coadded, ((0, 0), (0, 0), (radius, radius)))
    total = None
    for dy in range(KW):
        for dx in range(KW):
            tap = psf_kernel[:, dy * KW + dx][None, :, None]
            term = tap * padded[dy : dy + TROWS, :, dx : dx + columns].astype(F32)
            total = term if total is None else total + term
    return total.astype(BF16)


def body(
    exposure_pixels,
    block_band,
    block_tile,
    block_row,
    band_weights,
    psf_kernel,
    gal_tile,
    gal_row,
    gal_col,
    gal_shift,
):
    tile_count = lax.axis_size("tile")
    channels, columns = band_weights.shape[1], exposure_pixels.shape[2]
    gal_here = gal_tile.shape[0]
    depth = min(8, gal_here)
    span = 64
    tile_range = jnp.arange(tile_count, dtype=jnp.int32)
    row_range = jnp.arange(TROWS, dtype=jnp.int32)

    strip_range = jnp.arange(tile_count * TROWS, dtype=jnp.int32)
    target = block_tile * TROWS + block_row
    counts_out = jnp.sum((target[None, :] == strip_range[:, None]).astype(jnp.int32), axis=1)
    place = gal_tile * depth + rank_before(gal_tile)
    word = (gal_row * columns + gal_col) * span + gal_shift
    slot_range = jnp.arange(tile_count * depth, dtype=jnp.int32)
    words_out = jnp.sum(
        jnp.where(place[None, :] == slot_range[:, None], word[None, :], 0), axis=1
    )
    mine = (place[:, None] == slot_range[None, :]).astype(BF16)
    counts_out = counts_out.reshape(tile_count, TROWS)
    words_out = words_out.reshape(tile_count, depth)
    if tile_count == 16:
        return small_body(
            exposure_pixels, block_band, block_tile, block_row, band_weights, psf_kernel,
            counts_out, words_out, mine,
        )
    coadded, words = averaged_rows_any(
        exposure_pixels, block_band, block_tile, block_row, band_weights, counts_out, words_out
    )
    slot_shift = words % span
    slot_col = (words // span) % columns
    slot_row = words // (span * columns)
    matched_cube = psf_match(coadded, psf_kernel)

    column_range = jnp.arange(columns, dtype=jnp.int32)
    chosen = (
        (slot_row[None, None, :] == row_range[:, None, None])
        & (slot_col[None, None, :] == column_range[None, :, None])
    ).astype(BF16)
    spectra = lax.dot_general(
        matched_cube, chosen, (((0, 2), (0, 1)), ((), ())), preferred_element_type=F32
    )
    window = jnp.arange(NW, dtype=jnp.int32)
    channel_range = jnp.arange(channels, dtype=jnp.int32)
    inside = channel_range[None, :, None] == (slot_shift[None, :] + window[:, None])[:, None, :]
    values = jnp.sum(jnp.where(inside, spectra[None], 0.0), axis=1).T.astype(BF16)
    returned = lax.all_to_all(values, "tile", split_axis=0, concat_axis=0, tiled=True)
    rest_spectra = jnp.dot(mine, returned, preferred_element_type=F32).astype(BF16)
    return matched_cube, rest_spectra


def solution(mesh):
    one = P(("groups", "tile"))
    cube = P(("groups", "tile"), None, None)
    return jax.shard_map(
        body,
        mesh=mesh,
        in_specs=(cube, one, one, one, P(), P(), one, one, one, one),
        out_specs=(cube, P(("groups", "tile"), None)),
        check_vma=False,
    )
```

```python
import jax
import jax.numpy as jnp
from jax import lax
from jax.experimental import pallas as pl
from jax.experimental.pallas import tpu as pltpu
from jax.sharding import PartitionSpec as P

KW = 5
NW = 64
TROWS = 16
F32 = jnp.float32
BF16 = jnp.bfloat16
CHUNKS = 8
PART = TROWS // CHUNKS
SLAB = 4 * PART
ORDER = (0, 7, 1, 2, 3, 4, 5, 6)
MESH = pl.DeviceIdType.MESH
GROUP = 8


def partial_sums_kernel(
    place_ref, band_ref, pixels_hbm, weights_t_ref, keep_hbm, send_hbm,
    total, pixels_ref, weights_ref, keep_ref, send_ref, in_sem, out_sem,
):
    load = pltpu.make_async_copy(pixels_hbm, pixels_ref, in_sem)
    load.start()
    for band in range(weights_ref.shape[0]):
        weights_ref[band] = weights_t_ref[band].astype(F32).T.astype(BF16)
    blocks = pixels_ref.shape[0]
    half = total.shape[0] // 2

    def clear(i, _):
        total[i] = jnp.zeros(total.shape[1:], F32)
        return 0

    lax.fori_loop(0, total.shape[0], clear, 0, unroll=4)
    load.wait()

    def step(i, _):
        spectra = []
        for k in range(GROUP):
            b = i * GROUP + k
            spectra.append(
                jnp.dot(weights_ref[band_ref[b]], pixels_ref[b], preferred_element_type=F32)
            )
        for k in range(GROUP):
            b = i * GROUP + k
            total[place_ref[b]] += spectra[k].astype(BF16).astype(F32)
        return 0

    lax.fori_loop(0, blocks // GROUP, step, 0)

    copies = []
    for far in (1, 0):
        rows = pl.ds(far * half // 2, half // 2)
        for n, (buffer, out) in enumerate(((send_ref, send_hbm), (keep_ref, keep_hbm))):
            source = (half if n == 0 else 0) + far * half // 2

            def emit(i, _, buffer=buffer, source=source, far=far):
                buffer[far * half // 2 + i] = total[source + i].astype(BF16)
                return 0

            lax.fori_loop(0, half // 2, emit, 0, unroll=4)
            copy = pltpu.make_async_copy(buffer.at[rows], out.at[rows], out_sem.at[2 * far + n])
            copy.start()
            copies.append(copy)
    for copy in copies:
        copy.wait()


def partial_sums(place, band, pixels, weights, rows):
    channels, columns = weights.shape[1], pixels.shape[2]
    smem = pl.BlockSpec(memory_space=pltpu.SMEM)
    vmem = pl.BlockSpec(memory_space=pltpu.VMEM)
    return pl.pallas_call(
        partial_sums_kernel,
        out_shape=[jax.ShapeDtypeStruct((rows // 2, channels, columns), BF16)] * 2,
        in_specs=[smem, smem, pl.BlockSpec(memory_space=pl.ANY), vmem],
        out_specs=[pl.BlockSpec(memory_space=pl.ANY)] * 2,
        scratch_shapes=[
            pltpu.VMEM((rows, channels, columns), F32),
            pltpu.VMEM(pixels.shape, BF16),
            pltpu.VMEM(weights.shape, BF16),
            pltpu.VMEM((rows // 2, channels, columns), BF16),
            pltpu.VMEM((rows // 2, channels, columns), BF16),
            pltpu.SemaphoreType.DMA,
            pltpu.SemaphoreType.DMA((4,)),
        ],
        compiler_params=pltpu.CompilerParams(vmem_limit_bytes=28 * 1024 * 1024),
        name="partial_sums",
    )(place, band, pixels, jnp.swapaxes(weights, 1, 2))


def greet_all(me, count):
    barrier = pltpu.get_barrier_semaphore()

    def hello(k, _):
        pl.semaphore_signal(
            barrier, inc=1, device_id={"tile": (me + k) % count}, device_id_type=MESH
        )
        return 0

    lax.fori_loop(1, count, hello, 0)
    pl.semaphore_wait(barrier, count - 1)


def exchange_copy(k, me, count, out_ref, in_ref, send_sem, recv_sem):
    there = (me + k) % count
    return pltpu.make_async_remote_copy(
        src_ref=out_ref.at[there],
        dst_ref=in_ref.at[me],
        send_sem=send_sem.at[k],
        recv_sem=recv_sem.at[k],
        device_id={"tile": there},
        device_id_type=MESH,
    )


def reduce_kernel(
    notes_ref, keep_hbm, send_ref, psf_ref, mine_ref, cube_ref, rest_ref,
    notes_in, keep_ref, from_core, to_x, from_x, plane, chain_out, chain_in, halo_in, rows_ref,
    taps, picked, window_out, window_in,
    note_send, note_recv, window_send, window_recv, keep_sem, core_send, core_recv, x_send, x_recv,
    chain_send, chain_recv, halo_send, halo_recv,
):
    count = 16
    me = lax.axis_index("tile")
    z, x, c = me // 4, (me // 2) % 2, me % 2
    other_core = me + 1 - 2 * c
    other_x = me + 2 - 4 * x
    part, size = PART, SLAB
    channels, columns = cube_ref.shape[1], cube_ref.shape[2]

    def remote(src, dst, send_sem, recv_sem, there):
        return pltpu.make_async_remote_copy(
            src_ref=src, dst_ref=dst, send_sem=send_sem, recv_sem=recv_sem,
            device_id={"tile": there}, device_id_type=MESH,
        )

    def core_copy(far, k):
        at = far * CHUNKS + k
        rows = pl.ds(at * size, size)
        return remote(
            send_ref.at[rows], from_core.at[rows], core_send.at[at], core_recv.at[at], other_core
        )

    def x_copy(k):
        rows = pl.ds(k * size, size)
        return remote(to_x.at[rows], from_x.at[rows], x_send.at[k], x_recv.at[k], other_x)

    def chain_copy(way, k, dist):
        at = (way * CHUNKS + k) * 3 + dist - 1
        there = (me + 4) % count if way == 0 else (me + 12) % count
        rows = pl.ds(at * part, part)
        return remote(
            chain_out.at[rows], chain_in.at[rows], chain_send.at[at], chain_recv.at[at], there
        )

    def note(k):
        return exchange_copy(k, me, count, notes_ref, notes_in, note_send, note_recv)

    def window(k):
        return exchange_copy(k, me, count, window_out, window_in, window_send, window_recv)

    def keep_copy(far):
        rows = pl.ds(far * CHUNKS * size, CHUNKS * size)
        return pltpu.make_async_copy(keep_hbm.at[rows], keep_ref.at[rows], keep_sem.at[far])

    keep_copy(1).start()
    keep_copy(0).start()
    greet_all(me, count)
    for k in range(3):
        core_copy(1, k).start()

    def send_note(k, _):
        note(k).start()
        return 0

    lax.fori_loop(1, count, send_note, 0)

    def cross(k):
        core_copy(1, k).wait_recv()

        def add_x(i, _):
            at = (CHUNKS + k) * size + i
            to_x[k * size + i] = (
                keep_ref[at].astype(F32) + from_core[at].astype(F32)
            ).astype(BF16)
            return 0

        lax.fori_loop(0, size, add_x, 0, unroll=2)
        x_copy(k).start()

    keep_copy(1).wait()
    cross(0)
    core_copy(0, 0).start()
    cross(1)
    core_copy(0, 1).start()

    def wait_note(k, total):
        note(k).wait_recv()
        return total

    lax.fori_loop(1, count, wait_note, 0)
    notes_in[me] = notes_ref[me]
    keep_copy(0).wait()
    words = notes_in[:, TROWS:, :].reshape(-1, 128)
    slot_shift = words & 63
    slot_col = (words >> 6) & 127
    slot_row = words >> 13
    lane = lax.broadcasted_iota(jnp.int32, words.shape, 1)
    on_column = slot_col == lane
    picked[...] = jnp.zeros(picked.shape, F32)
    psf = psf_ref[...].T
    for tap in range(KW * KW):
        taps[tap] = jnp.broadcast_to(psf[:, tap : tap + 1], (channels, columns))
    counts = jnp.maximum(jnp.sum(notes_in[:, :TROWS, :], axis=0).astype(F32), 1.0)

    def sends(way, dist):
        return z + dist <= 3 if way == 0 else z >= dist

    def receives(way, dist):
        if way == 0:
            return jnp.logical_and(z >= 1, z + dist <= 4)
        return jnp.logical_and(z <= 2, z >= dist - 1)

    def hop(k, dist):
        for way in range(2):

            @pl.when(sends(way, dist))
            def _(way=way):
                to_z = z + dist if way == 0 else z - dist
                at = ((way * CHUNKS + k) * 3 + dist - 1) * part
                source = k * size + to_z * part
                edge = z >= 1 if way == 0 else z <= 2
                if dist == 3:
                    def put(i, _):
                        chain_out[at + i] = plane[source + i]
                        return 0

                    lax.fori_loop(0, part, put, 0)
                else:
                    @pl.when(edge)
                    def _():
                        chain_copy(way, k, dist + 1).wait_recv()

                        def put(i, _):
                            chain_out[at + i] = (
                                plane[source + i].astype(F32)
                                + chain_in[at + part + i].astype(F32)
                            ).astype(BF16)
                            return 0

                        lax.fori_loop(0, part, put, 0)

                    @pl.when(jnp.logical_not(edge))
                    def _():
                        def put(i, _):
                            chain_out[at + i] = plane[source + i]
                            return 0

                        lax.fori_loop(0, part, put, 0)
                chain_copy(way, k, dist).start()

    def finish(k):
        up_at, down_at = k * 3 * part, (CHUNKS + k) * 3 * part

        @pl.when(receives(0, 1))
        def _():
            chain_copy(0, k, 1).wait_recv()

        @pl.when(receives(1, 1))
        def _():
            chain_copy(1, k, 1).wait_recv()

        up_on, down_on = z >= 1, z <= 2
        for i in range(part):
            value = plane[k * size + z * part + i].astype(F32)
            value = value + jnp.where(up_on, chain_in[up_at + i].astype(F32), 0.0)
            value = value + jnp.where(down_on, chain_in[down_at + i].astype(F32), 0.0)
            row = ORDER[k] * part + i
            rows_ref[2 + row] = (value / counts[row : row + 1, :]).astype(BF16)

    def halo_copy(way):
        rows = pl.ds(2, 2) if way == 0 else pl.ds(TROWS, 2)
        there = (me + 15) % count if way == 0 else (me + 1) % count
        return remote(
            rows_ref.at[rows], halo_in.at[pl.ds(2 * way, 2)], halo_send.at[way],
            halo_recv.at[way], there,
        )

    def match_row(y, _):
        radius = KW // 2
        near = [rows_ref[y + dy].astype(F32) for dy in range(KW)]
        at = lax.broadcasted_iota(jnp.int32, (channels, columns), 1)
        total = None
        for dx in range(KW):
            term = taps[dx] * near[0]
            for dy in range(1, KW):
                term = term + taps[dy * KW + dx] * near[dy]
            offset = dx - radius
            if offset != 0:
                term = pltpu.roll(term, (-offset) % columns, 1)
                valid = at < columns - offset if offset > 0 else at >= -offset
                term = jnp.where(valid, term, 0.0)
            total = term if total is None else total + term
        matched = total.astype(BF16)
        cube_ref[y] = matched
        chosen = jnp.where(jnp.logical_and(on_column, slot_row == y), 1.0, 0.0).astype(BF16)
        picked[:, :channels] += lax.dot_general(
            chosen, matched, (((1,), (1,)), ((), ())), preferred_element_type=F32
        )
        return 0

    def take_halo():
        @pl.when(me <= count - 2)
        def _():
            halo_copy(0).wait_recv()
            for i in range(2):
                rows_ref[TROWS + 2 + i] = halo_in[i]

        @pl.when(me >= 1)
        def _():
            halo_copy(1).wait_recv()
            for i in range(2):
                rows_ref[i] = halo_in[2 + i]

    def done(k):
        finish(k)
        if k == 0:
            @pl.when(me >= 1)
            def _():
                halo_copy(0).start()
        if k == 1:
            @pl.when(me <= count - 2)
            def _():
                halo_copy(1).start()
        if k == 4:
            take_halo()
            lax.fori_loop(0, 2, match_row, 0)
        if k >= 3:
            lax.fori_loop(2 * k - 4, 2 * k - 2 if k < CHUNKS - 1 else TROWS, match_row, 0)

    for i in range(2):
        rows_ref[i] = jnp.zeros(rows_ref.shape[1:], BF16)
        rows_ref[TROWS + 2 + i] = jnp.zeros(rows_ref.shape[1:], BF16)

    for t in range(CHUNKS + 3):
        if t < CHUNKS:
            x_copy(t).wait_recv()
            if t + 2 < CHUNKS:
                cross(t + 2)
                core_copy(0, t + 2).start()
            if t + 3 < CHUNKS:
                core_copy(1, t + 3).start()
            core_copy(0, t).wait_recv()

            def add_plane(i, _, t=t):
                at = t * size + i
                plane[at] = (
                    keep_ref[at].astype(F32) + from_core[at].astype(F32) + from_x[at].astype(F32)
                ).astype(BF16)
                return 0

            lax.fori_loop(0, size, add_plane, 0, unroll=2)
            hop(t, 3)
        if 0 <= t - 1 < CHUNKS:
            hop(t - 1, 2)
        if 0 <= t - 2 < CHUNKS:
            hop(t - 2, 1)
        if t >= 3:
            done(t - 3)

    chosen_window = picked[...]
    for bit in range(6):
        moved = pltpu.roll(chosen_window, 128 - 2**bit, 1)
        chosen_window = jnp.where((slot_shift >> bit) & 1 == 1, moved, chosen_window)
    window_out[...] = chosen_window.reshape(window_out.shape)

    def send_window(k, _):
        window(k).start()
        return 0

    def take_window(k, _):
        window(k).wait()
        return 0

    lax.fori_loop(1, count, send_window, 0)
    window_in[me] = window_out[me]

    @pl.when(me >= 1)
    def _():
        halo_copy(0).wait_send()

    @pl.when(me <= count - 2)
    def _():
        halo_copy(1).wait_send()

    def wait_note_sent(k, _):
        note(k).wait_send()
        return 0

    lax.fori_loop(1, count, wait_note_sent, 0)
    for k in range(CHUNKS):
        core_copy(1, k).wait_send()
        core_copy(0, k).wait_send()
        x_copy(k).wait_send()
        for way in range(2):
            for dist in (3, 2, 1):
                @pl.when(sends(way, dist))
                def _(way=way, k=k, dist=dist):
                    chain_copy(way, k, dist).wait_send()
    lax.fori_loop(1, count, take_window, 0)
    landed = window_in[...].reshape(-1, 128).astype(BF16)
    rest = jnp.dot(mine_ref[...], landed, preferred_element_type=F32)
    rest_ref[...] = rest[:, :NW].astype(BF16)


def reduce_and_match(notes, keep, send, psf_kernel, mine):
    tail = keep.shape[1:]
    vmem = pl.BlockSpec(memory_space=pltpu.VMEM)
    hbm = pl.BlockSpec(memory_space=pl.ANY)
    dma = pltpu.SemaphoreType.DMA
    slots = mine.shape[1]
    return pl.pallas_call(
        reduce_kernel,
        out_shape=[
            jax.ShapeDtypeStruct((TROWS,) + tail, BF16),
            jax.ShapeDtypeStruct((mine.shape[0], NW), BF16),
        ],
        in_specs=[vmem, hbm, hbm, vmem, vmem],
        out_specs=[vmem] * 2,
        scratch_shapes=[
            pltpu.VMEM(notes.shape, jnp.int32),
            pltpu.VMEM((8 * TROWS,) + tail, BF16),
            pltpu.VMEM((8 * TROWS,) + tail, BF16),
            pltpu.VMEM((4 * TROWS,) + tail, BF16),
            pltpu.VMEM((4 * TROWS,) + tail, BF16),
            pltpu.VMEM((4 * TROWS,) + tail, BF16),
            pltpu.VMEM((6 * TROWS,) + tail, BF16),
            pltpu.VMEM((6 * TROWS,) + tail, BF16),
            pltpu.VMEM((4,) + tail, BF16),
            pltpu.VMEM((TROWS + 4,) + tail, BF16),
            pltpu.VMEM((KW * KW,) + tail, F32),
            pltpu.VMEM((slots, 128), F32),
            pltpu.VMEM((16, slots // 16, 128), F32),
            pltpu.VMEM((16, slots // 16, 128), F32),
            dma((16,)), dma((16,)), dma((16,)), dma((16,)), dma((2,)),
            dma((2 * CHUNKS,)), dma((2 * CHUNKS,)),
            dma((CHUNKS,)), dma((CHUNKS,)),
            dma((6 * CHUNKS,)), dma((6 * CHUNKS,)),
            dma((2,)), dma((2,)),
        ],
        compiler_params=pltpu.CompilerParams(
            collective_id=0, has_side_effects=True, vmem_limit_bytes=28 * 1024 * 1024
        ),
        name="reduce_and_match",
    )(notes, keep, send, psf_kernel.T, mine)


def small_body(pixels, band, tile, row, weights, psf_kernel, counts_out, words_out, mine):
    me = lax.axis_index("tile")
    x, c = (me // 2) % 2, me % 2
    dest_z, dest_x, dest_c = tile // 4, (tile // 2) % 2, tile % 2
    far_x, far_c = (dest_x + x) % 2, (dest_c + c) % 2
    pair = row // PART
    chunk = jnp.where(pair == 0, 0, jnp.where(pair == CHUNKS - 1, 1, pair + 1))
    place = (((far_c * 2 + far_x) * CHUNKS + chunk) * 4 + dest_z) * PART + row % PART
    keep, send = partial_sums(place, band, pixels, weights, 16 * TROWS)
    notes = jnp.concatenate([counts_out, words_out], axis=1)
    notes = jnp.broadcast_to(notes[:, :, None], notes.shape + (128,))
    return reduce_and_match(notes, keep, send, psf_kernel, mine)


def averaged_rows_any(pixels, band, tile, row, weights, counts_out, words_out):
    sent = jnp.concatenate([counts_out, words_out], axis=1)
    got = lax.all_to_all(sent, "tile", split_axis=0, concat_axis=0, tiled=True)
    counts = jnp.sum(got[:, :TROWS], axis=0).astype(F32)
    row_sums = tile_row_sums_any(pixels, band, tile, row, weights)
    rows = (row_sums / jnp.maximum(counts, 1.0)[:, None, None]).astype(BF16)
    return with_halo(rows, KW // 2), got[:, TROWS:].reshape(-1)


def tile_row_sums_any(pixels, band, tile, row, weights):
    tile_count = lax.axis_size("tile")
    blocks = pixels.shape[0]
    capacity = 2 * blocks // tile_count
    slots = tile_count * capacity
    place = tile * capacity + rank_before(tile)
    tag = jnp.full((slots,), -1, jnp.int32).at[place].set(row * weights.shape[0] + band)
    packed = jnp.zeros((slots,) + pixels.shape[1:], BF16).at[place].set(pixels)
    packed = lax.all_to_all(packed, "tile", split_axis=0, concat_axis=0, tiled=True)
    tag = lax.all_to_all(tag, "tile", split_axis=0, concat_axis=0, tiled=True)
    bands = jnp.maximum(tag, 0) % weights.shape[0]
    rows = jnp.where(tag < 0, -1, tag // weights.shape[0])
    spectra = jnp.einsum("bcs,bsp->bcp", weights[bands], packed, preferred_element_type=F32)
    spectra = spectra.astype(BF16).reshape(slots, -1)
    table = (rows[None, :] == jnp.arange(TROWS)[:, None]).astype(BF16)
    sums = jnp.dot(table, spectra, preferred_element_type=F32)
    return sums.reshape(TROWS, weights.shape[1], pixels.shape[2])


def rank_before(tiles):
    positions = jnp.arange(tiles.shape[0], dtype=jnp.int32)
    earlier = (tiles[:, None] == tiles[None, :]) & (positions[None, :] < positions[:, None])
    return jnp.sum(earlier.astype(jnp.int32), axis=-1)


def with_halo(cells, width):
    count = lax.axis_size("tile")
    ends = count - 1
    above = lax.ppermute(cells[-width:], "tile", [(i, i + 1) for i in range(ends)])
    below = lax.ppermute(cells[:width], "tile", [(i + 1, i) for i in range(ends)])
    return jnp.concatenate([above, cells, below], axis=0)


def psf_match(coadded, psf_kernel):
    radius = KW // 2
    columns = coadded.shape[2]
    padded = jnp.pad(coadded, ((0, 0), (0, 0), (radius, radius)))
    total = None
    for dy in range(KW):
        for dx in range(KW):
            tap = psf_kernel[:, dy * KW + dx][None, :, None]
            term = tap * padded[dy : dy + TROWS, :, dx : dx + columns].astype(F32)
            total = term if total is None else total + term
    return total.astype(BF16)


def body(
    exposure_pixels,
    block_band,
    block_tile,
    block_row,
    band_weights,
    psf_kernel,
    gal_tile,
    gal_row,
    gal_col,
    gal_shift,
):
    tile_count = lax.axis_size("tile")
    channels, columns = band_weights.shape[1], exposure_pixels.shape[2]
    gal_here = gal_tile.shape[0]
    depth = min(8, gal_here)
    span = 64
    tile_range = jnp.arange(tile_count, dtype=jnp.int32)
    row_range = jnp.arange(TROWS, dtype=jnp.int32)

    strip_range = jnp.arange(tile_count * TROWS, dtype=jnp.int32)
    target = block_tile * TROWS + block_row
    counts_out = jnp.sum((target[None, :] == strip_range[:, None]).astype(jnp.int32), axis=1)
    place = gal_tile * depth + rank_before(gal_tile)
    word = (gal_row * columns + gal_col) * span + gal_shift
    slot_range = jnp.arange(tile_count * depth, dtype=jnp.int32)
    words_out = jnp.sum(
        jnp.where(place[None, :] == slot_range[:, None], word[None, :], 0), axis=1
    )
    mine = (place[:, None] == slot_range[None, :]).astype(BF16)
    counts_out = counts_out.reshape(tile_count, TROWS)
    words_out = words_out.reshape(tile_count, depth)
    if tile_count == 16:
        return small_body(
            exposure_pixels, block_band, block_tile, block_row, band_weights, psf_kernel,
            counts_out, words_out, mine,
        )
    coadded, words = averaged_rows_any(
        exposure_pixels, block_band, block_tile, block_row, band_weights, counts_out, words_out
    )
    slot_shift = words % span
    slot_col = (words // span) % columns
    slot_row = words // (span * columns)
    matched_cube = psf_match(coadded, psf_kernel)

    column_range = jnp.arange(columns, dtype=jnp.int32)
    chosen = (
        (slot_row[None, None, :] == row_range[:, None, None])
        & (slot_col[None, None, :] == column_range[None, :, None])
    ).astype(BF16)
    spectra = lax.dot_general(
        matched_cube, chosen, (((0, 2), (0, 1)), ((), ())), preferred_element_type=F32
    )
    window = jnp.arange(NW, dtype=jnp.int32)
    channel_range = jnp.arange(channels, dtype=jnp.int32)
    inside = channel_range[None, :, None] == (slot_shift[None, :] + window[:, None])[:, None, :]
    values = jnp.sum(jnp.where(inside, spectra[None], 0.0), axis=1).T.astype(BF16)
    returned = lax.all_to_all(values, "tile", split_axis=0, concat_axis=0, tiled=True)
    rest_spectra = jnp.dot(mine, returned, preferred_element_type=F32).astype(BF16)
    return matched_cube, rest_spectra


def solution(mesh):
    one = P(("groups", "tile"))
    cube = P(("groups", "tile"), None, None)
    return jax.shard_map(
        body,
        mesh=mesh,
        in_specs=(cube, one, one, one, P(), P(), one, one, one, one),
        out_specs=(cube, P(("groups", "tile"), None)),
        check_vma=False,
    )
```

```python
import jax
import jax.numpy as jnp
from jax import lax
from jax.experimental import pallas as pl
from jax.experimental.pallas import tpu as pltpu
from jax.sharding import PartitionSpec as P

KW = 5
NW = 64
TROWS = 16
F32 = jnp.float32
BF16 = jnp.bfloat16
CHUNKS = 8
PART = TROWS // CHUNKS
SLAB = 4 * PART


def padded_channels(channels):
    return -(-channels // 8) * 8

ORDER = (0, 7, 1, 2, 3, 4, 5, 6)
MESH = pl.DeviceIdType.MESH
GROUP = 8


def partial_sums_kernel(
    place_ref, band_ref, pixels_hbm, weights_t_ref, keep_hbm, send_hbm,
    total, pixels_ref, weights_ref, keep_ref, send_ref, in_sem, out_sem,
):
    load = pltpu.make_async_copy(pixels_hbm, pixels_ref, in_sem)
    load.start()
    weights_ref[...] = jnp.zeros(weights_ref.shape, BF16)
    for band in range(weights_ref.shape[0]):
        weights_ref[band, : weights_t_ref.shape[2]] = (
            weights_t_ref[band].astype(F32).T.astype(BF16)
        )
    blocks = pixels_ref.shape[0]
    half = total.shape[0] // 2

    def clear(i, _):
        total[i] = jnp.zeros(total.shape[1:], F32)
        return 0

    lax.fori_loop(0, total.shape[0], clear, 0, unroll=4)
    load.wait()

    def step(i, _):
        spectra = []
        for k in range(GROUP):
            b = i * GROUP + k
            spectra.append(
                jnp.dot(weights_ref[band_ref[b]], pixels_ref[b], preferred_element_type=F32)
            )
        for k in range(GROUP):
            b = i * GROUP + k
            total[place_ref[b]] += spectra[k].astype(BF16).astype(F32)
        return 0

    lax.fori_loop(0, blocks // GROUP, step, 0)

    copies = []
    for far in (1, 0):
        rows = pl.ds(far * half // 2, half // 2)
        for n, (buffer, out) in enumerate(((send_ref, send_hbm), (keep_ref, keep_hbm))):
            source = (half if n == 0 else 0) + far * half // 2

            def emit(i, _, buffer=buffer, source=source, far=far):
                buffer[far * half // 2 + i] = total[source + i].astype(BF16)
                return 0

            lax.fori_loop(0, half // 2, emit, 0, unroll=4)
            copy = pltpu.make_async_copy(buffer.at[rows], out.at[rows], out_sem.at[2 * far + n])
            copy.start()
            copies.append(copy)
    for copy in copies:
        copy.wait()


def partial_sums(place, band, pixels, weights, rows):
    channels, columns = padded_channels(weights.shape[1]), pixels.shape[2]
    smem = pl.BlockSpec(memory_space=pltpu.SMEM)
    vmem = pl.BlockSpec(memory_space=pltpu.VMEM)
    return pl.pallas_call(
        partial_sums_kernel,
        out_shape=[jax.ShapeDtypeStruct((rows // 2, channels, columns), BF16)] * 2,
        in_specs=[smem, smem, pl.BlockSpec(memory_space=pl.ANY), vmem],
        out_specs=[pl.BlockSpec(memory_space=pl.ANY)] * 2,
        scratch_shapes=[
            pltpu.VMEM((rows, channels, columns), F32),
            pltpu.VMEM(pixels.shape, BF16),
            pltpu.VMEM((weights.shape[0], channels, weights.shape[2]), BF16),
            pltpu.VMEM((rows // 2, channels, columns), BF16),
            pltpu.VMEM((rows // 2, channels, columns), BF16),
            pltpu.SemaphoreType.DMA,
            pltpu.SemaphoreType.DMA((4,)),
        ],
        compiler_params=pltpu.CompilerParams(vmem_limit_bytes=28 * 1024 * 1024),
        name="partial_sums",
    )(place, band, pixels, jnp.swapaxes(weights, 1, 2))


def greet_all(me, count):
    barrier = pltpu.get_barrier_semaphore()

    def hello(k, _):
        pl.semaphore_signal(
            barrier, inc=1, device_id={"tile": (me + k) % count}, device_id_type=MESH
        )
        return 0

    lax.fori_loop(1, count, hello, 0)
    pl.semaphore_wait(barrier, count - 1)


def exchange_copy(k, me, count, out_ref, in_ref, send_sem, recv_sem):
    there = (me + k) % count
    return pltpu.make_async_remote_copy(
        src_ref=out_ref.at[there],
        dst_ref=in_ref.at[me],
        send_sem=send_sem.at[k],
        recv_sem=recv_sem.at[k],
        device_id={"tile": there},
        device_id_type=MESH,
    )


def reduce_kernel(
    notes_ref, keep_hbm, send_ref, psf_ref, mine_ref, cube_ref, rest_ref,
    notes_in, keep_ref, from_core, to_x, from_x, plane, chain_out, chain_in, halo_in, rows_ref,
    taps, picked, window_out, window_in,
    note_send, note_recv, window_send, window_recv, keep_sem, core_send, core_recv, x_send, x_recv,
    chain_send, chain_recv, halo_send, halo_recv,
):
    count = 16
    me = lax.axis_index("tile")
    z, x, c = me // 4, (me // 2) % 2, me % 2
    other_core = me + 1 - 2 * c
    other_x = me + 2 - 4 * x
    part, size = PART, SLAB
    channels, columns = rows_ref.shape[1], rows_ref.shape[2]
    used = cube_ref.shape[1]

    def remote(src, dst, send_sem, recv_sem, there):
        return pltpu.make_async_remote_copy(
            src_ref=src, dst_ref=dst, send_sem=send_sem, recv_sem=recv_sem,
            device_id={"tile": there}, device_id_type=MESH,
        )

    def core_copy(far, k):
        at = far * CHUNKS + k
        rows = pl.ds(at * size, size)
        return remote(
            send_ref.at[rows], from_core.at[rows], core_send.at[at], core_recv.at[at], other_core
        )

    def x_copy(k):
        rows = pl.ds(k * size, size)
        return remote(to_x.at[rows], from_x.at[rows], x_send.at[k], x_recv.at[k], other_x)

    def chain_copy(way, k, dist):
        at = (way * CHUNKS + k) * 3 + dist - 1
        there = (me + 4) % count if way == 0 else (me + 12) % count
        rows = pl.ds(at * part, part)
        return remote(
            chain_out.at[rows], chain_in.at[rows], chain_send.at[at], chain_recv.at[at], there
        )

    def note(k):
        return exchange_copy(k, me, count, notes_ref, notes_in, note_send, note_recv)

    def window(k):
        return exchange_copy(k, me, count, window_out, window_in, window_send, window_recv)

    def keep_copy(far):
        rows = pl.ds(far * CHUNKS * size, CHUNKS * size)
        return pltpu.make_async_copy(keep_hbm.at[rows], keep_ref.at[rows], keep_sem.at[far])

    keep_copy(1).start()
    keep_copy(0).start()
    greet_all(me, count)
    for k in range(3):
        core_copy(1, k).start()

    def send_note(k, _):
        note(k).start()
        return 0

    lax.fori_loop(1, count, send_note, 0)

    def cross(k):
        core_copy(1, k).wait_recv()

        def add_x(i, _):
            at = (CHUNKS + k) * size + i
            to_x[k * size + i] = (
                keep_ref[at].astype(F32) + from_core[at].astype(F32)
            ).astype(BF16)
            return 0

        lax.fori_loop(0, size, add_x, 0, unroll=2)
        x_copy(k).start()

    keep_copy(1).wait()
    cross(0)
    core_copy(0, 0).start()
    cross(1)
    core_copy(0, 1).start()

    def wait_note(k, total):
        note(k).wait_recv()
        return total

    lax.fori_loop(1, count, wait_note, 0)
    notes_in[me] = notes_ref[me]
    keep_copy(0).wait()
    words = notes_in[:, TROWS:, :].reshape(-1, 128)
    slot_shift = words & 63
    slot_col = (words >> 6) & 127
    slot_row = words >> 13
    lane = lax.broadcasted_iota(jnp.int32, words.shape, 1)
    on_column = slot_col == lane
    picked[...] = jnp.zeros(picked.shape, F32)
    psf = psf_ref[...].T
    taps[...] = jnp.zeros(taps.shape, F32)
    for tap in range(KW * KW):
        taps[tap, :used] = jnp.broadcast_to(psf[:, tap : tap + 1], (used, columns))
    counts = jnp.maximum(jnp.sum(notes_in[:, :TROWS, :], axis=0).astype(F32), 1.0)

    def sends(way, dist):
        return z + dist <= 3 if way == 0 else z >= dist

    def receives(way, dist):
        if way == 0:
            return jnp.logical_and(z >= 1, z + dist <= 4)
        return jnp.logical_and(z <= 2, z >= dist - 1)

    def hop(k, dist):
        for way in range(2):

            @pl.when(sends(way, dist))
            def _(way=way):
                to_z = z + dist if way == 0 else z - dist
                at = ((way * CHUNKS + k) * 3 + dist - 1) * part
                source = k * size + to_z * part
                edge = z >= 1 if way == 0 else z <= 2
                if dist == 3:
                    def put(i, _):
                        chain_out[at + i] = plane[source + i]
                        return 0

                    lax.fori_loop(0, part, put, 0)
                else:
                    @pl.when(edge)
                    def _():
                        chain_copy(way, k, dist + 1).wait_recv()

                        def put(i, _):
                            chain_out[at + i] = (
                                plane[source + i].astype(F32)
                                + chain_in[at + part + i].astype(F32)
                            ).astype(BF16)
                            return 0

                        lax.fori_loop(0, part, put, 0)

                    @pl.when(jnp.logical_not(edge))
                    def _():
                        def put(i, _):
                            chain_out[at + i] = plane[source + i]
                            return 0

                        lax.fori_loop(0, part, put, 0)
                chain_copy(way, k, dist).start()

    def finish(k):
        up_at, down_at = k * 3 * part, (CHUNKS + k) * 3 * part

        @pl.when(receives(0, 1))
        def _():
            chain_copy(0, k, 1).wait_recv()

        @pl.when(receives(1, 1))
        def _():
            chain_copy(1, k, 1).wait_recv()

        up_on, down_on = z >= 1, z <= 2
        for i in range(part):
            value = plane[k * size + z * part + i].astype(F32)
            value = value + jnp.where(up_on, chain_in[up_at + i].astype(F32), 0.0)
            value = value + jnp.where(down_on, chain_in[down_at + i].astype(F32), 0.0)
            row = ORDER[k] * part + i
            rows_ref[2 + row] = (value / counts[row : row + 1, :]).astype(BF16)

    def halo_copy(way):
        rows = pl.ds(2, 2) if way == 0 else pl.ds(TROWS, 2)
        there = (me + 15) % count if way == 0 else (me + 1) % count
        return remote(
            rows_ref.at[rows], halo_in.at[pl.ds(2 * way, 2)], halo_send.at[way],
            halo_recv.at[way], there,
        )

    def match_row(y, _):
        radius = KW // 2
        near = [rows_ref[y + dy].astype(F32) for dy in range(KW)]
        at = lax.broadcasted_iota(jnp.int32, (channels, columns), 1)
        total = None
        for dx in range(KW):
            term = taps[dx] * near[0]
            for dy in range(1, KW):
                term = term + taps[dy * KW + dx] * near[dy]
            offset = dx - radius
            if offset != 0:
                term = pltpu.roll(term, (-offset) % columns, 1)
                valid = at < columns - offset if offset > 0 else at >= -offset
                term = jnp.where(valid, term, 0.0)
            total = term if total is None else total + term
        matched = total.astype(BF16)
        cube_ref[y] = matched[:used]
        chosen = jnp.where(jnp.logical_and(on_column, slot_row == y), 1.0, 0.0).astype(BF16)
        picked[:, :channels] += lax.dot_general(
            chosen, matched, (((1,), (1,)), ((), ())), preferred_element_type=F32
        )
        return 0

    def take_halo():
        @pl.when(me <= count - 2)
        def _():
            halo_copy(0).wait_recv()
            for i in range(2):
                rows_ref[TROWS + 2 + i] = halo_in[i]

        @pl.when(me >= 1)
        def _():
            halo_copy(1).wait_recv()
            for i in range(2):
                rows_ref[i] = halo_in[2 + i]

    def done(k):
        finish(k)
        if k == 0:
            @pl.when(me >= 1)
            def _():
                halo_copy(0).start()
        if k == 1:
            @pl.when(me <= count - 2)
            def _():
                halo_copy(1).start()
        if k == 4:
            take_halo()
            lax.fori_loop(0, 2, match_row, 0)
        if k >= 3:
            lax.fori_loop(2 * k - 4, 2 * k - 2 if k < CHUNKS - 1 else TROWS, match_row, 0)

    for i in range(2):
        rows_ref[i] = jnp.zeros(rows_ref.shape[1:], BF16)
        rows_ref[TROWS + 2 + i] = jnp.zeros(rows_ref.shape[1:], BF16)

    for t in range(CHUNKS + 3):
        if t < CHUNKS:
            x_copy(t).wait_recv()
            if t + 2 < CHUNKS:
                cross(t + 2)
                core_copy(0, t + 2).start()
            if t + 3 < CHUNKS:
                core_copy(1, t + 3).start()
            core_copy(0, t).wait_recv()

            def add_plane(i, _, t=t):
                at = t * size + i
                plane[at] = (
                    keep_ref[at].astype(F32) + from_core[at].astype(F32) + from_x[at].astype(F32)
                ).astype(BF16)
                return 0

            lax.fori_loop(0, size, add_plane, 0, unroll=2)
            hop(t, 3)
        if 0 <= t - 1 < CHUNKS:
            hop(t - 1, 2)
        if 0 <= t - 2 < CHUNKS:
            hop(t - 2, 1)
        if t >= 3:
            done(t - 3)

    chosen_window = picked[...]
    for bit in range(6):
        moved = pltpu.roll(chosen_window, 128 - 2**bit, 1)
        chosen_window = jnp.where((slot_shift >> bit) & 1 == 1, moved, chosen_window)
    window_out[...] = chosen_window.reshape(window_out.shape)

    def send_window(k, _):
        window(k).start()
        return 0

    def take_window(k, _):
        window(k).wait()
        return 0

    lax.fori_loop(1, count, send_window, 0)
    window_in[me] = window_out[me]

    @pl.when(me >= 1)
    def _():
        halo_copy(0).wait_send()

    @pl.when(me <= count - 2)
    def _():
        halo_copy(1).wait_send()

    def wait_note_sent(k, _):
        note(k).wait_send()
        return 0

    lax.fori_loop(1, count, wait_note_sent, 0)
    for k in range(CHUNKS):
        core_copy(1, k).wait_send()
        core_copy(0, k).wait_send()
        x_copy(k).wait_send()
        for way in range(2):
            for dist in (3, 2, 1):
                @pl.when(sends(way, dist))
                def _(way=way, k=k, dist=dist):
                    chain_copy(way, k, dist).wait_send()
    lax.fori_loop(1, count, take_window, 0)
    landed = window_in[...].reshape(-1, 128).astype(BF16)
    rest = jnp.dot(mine_ref[...], landed, preferred_element_type=F32)
    rest_ref[...] = rest[:, :NW].astype(BF16)


def reduce_and_match(notes, keep, send, psf_t, mine):
    tail = keep.shape[1:]
    vmem = pl.BlockSpec(memory_space=pltpu.VMEM)
    hbm = pl.BlockSpec(memory_space=pl.ANY)
    dma = pltpu.SemaphoreType.DMA
    slots = mine.shape[1]
    return pl.pallas_call(
        reduce_kernel,
        out_shape=[
            jax.ShapeDtypeStruct((TROWS, psf_t.shape[1], tail[1]), BF16),
            jax.ShapeDtypeStruct((mine.shape[0], NW), BF16),
        ],
        in_specs=[vmem, hbm, hbm, vmem, vmem],
        out_specs=[vmem] * 2,
        scratch_shapes=[
            pltpu.VMEM(notes.shape, jnp.int32),
            pltpu.VMEM((8 * TROWS,) + tail, BF16),
            pltpu.VMEM((8 * TROWS,) + tail, BF16),
            pltpu.VMEM((4 * TROWS,) + tail, BF16),
            pltpu.VMEM((4 * TROWS,) + tail, BF16),
            pltpu.VMEM((4 * TROWS,) + tail, BF16),
            pltpu.VMEM((6 * TROWS,) + tail, BF16),
            pltpu.VMEM((6 * TROWS,) + tail, BF16),
            pltpu.VMEM((4,) + tail, BF16),
            pltpu.VMEM((TROWS + 4,) + tail, BF16),
            pltpu.VMEM((KW * KW,) + tail, F32),
            pltpu.VMEM((slots, 128), F32),
            pltpu.VMEM((16, slots // 16, 128), F32),
            pltpu.VMEM((16, slots // 16, 128), F32),
            dma((16,)), dma((16,)), dma((16,)), dma((16,)), dma((2,)),
            dma((2 * CHUNKS,)), dma((2 * CHUNKS,)),
            dma((CHUNKS,)), dma((CHUNKS,)),
            dma((6 * CHUNKS,)), dma((6 * CHUNKS,)),
            dma((2,)), dma((2,)),
        ],
        compiler_params=pltpu.CompilerParams(
            collective_id=0, has_side_effects=True, vmem_limit_bytes=28 * 1024 * 1024
        ),
        name="reduce_and_match",
    )(notes, keep, send, psf_t, mine)


def small_body(pixels, band, tile, row, weights, psf_kernel, counts_out, words_out, mine):
    me = lax.axis_index("tile")
    x, c = (me // 2) % 2, me % 2
    dest_z, dest_x, dest_c = tile // 4, (tile // 2) % 2, tile % 2
    far_x, far_c = (dest_x + x) % 2, (dest_c + c) % 2
    pair = row // PART
    chunk = jnp.where(pair == 0, 0, jnp.where(pair == CHUNKS - 1, 1, pair + 1))
    place = (((far_c * 2 + far_x) * CHUNKS + chunk) * 4 + dest_z) * PART + row % PART
    keep, send = partial_sums(place, band, pixels, weights, 16 * TROWS)
    notes = jnp.concatenate([counts_out, words_out], axis=1)
    notes = jnp.broadcast_to(notes[:, :, None], notes.shape + (128,))
    return reduce_and_match(notes, keep, send, psf_kernel.T, mine)


def averaged_rows_any(pixels, band, tile, row, weights, counts_out, words_out):
    sent = jnp.concatenate([counts_out, words_out], axis=1)
    got = lax.all_to_all(sent, "tile", split_axis=0, concat_axis=0, tiled=True)
    counts = jnp.sum(got[:, :TROWS], axis=0).astype(F32)
    row_sums = tile_row_sums_any(pixels, band, tile, row, weights)
    rows = (row_sums / jnp.maximum(counts, 1.0)[:, None, None]).astype(BF16)
    return with_halo(rows, KW // 2), got[:, TROWS:].reshape(-1)


def tile_row_sums_any(pixels, band, tile, row, weights):
    tile_count = lax.axis_size("tile")
    blocks = pixels.shape[0]
    capacity = 2 * blocks // tile_count
    slots = tile_count * capacity
    place = tile * capacity + rank_before(tile)
    tag = jnp.full((slots,), -1, jnp.int32).at[place].set(row * weights.shape[0] + band)
    packed = jnp.zeros((slots,) + pixels.shape[1:], BF16).at[place].set(pixels)
    packed = lax.all_to_all(packed, "tile", split_axis=0, concat_axis=0, tiled=True)
    tag = lax.all_to_all(tag, "tile", split_axis=0, concat_axis=0, tiled=True)
    bands = jnp.maximum(tag, 0) % weights.shape[0]
    rows = jnp.where(tag < 0, -1, tag // weights.shape[0])
    spectra = jnp.einsum("bcs,bsp->bcp", weights[bands], packed, preferred_element_type=F32)
    spectra = spectra.astype(BF16).reshape(slots, -1)
    table = (rows[None, :] == jnp.arange(TROWS)[:, None]).astype(BF16)
    sums = jnp.dot(table, spectra, preferred_element_type=F32)
    return sums.reshape(TROWS, weights.shape[1], pixels.shape[2])


def rank_before(tiles):
    positions = jnp.arange(tiles.shape[0], dtype=jnp.int32)
    earlier = (tiles[:, None] == tiles[None, :]) & (positions[None, :] < positions[:, None])
    return jnp.sum(earlier.astype(jnp.int32), axis=-1)


def with_halo(cells, width):
    count = lax.axis_size("tile")
    ends = count - 1
    above = lax.ppermute(cells[-width:], "tile", [(i, i + 1) for i in range(ends)])
    below = lax.ppermute(cells[:width], "tile", [(i + 1, i) for i in range(ends)])
    return jnp.concatenate([above, cells, below], axis=0)


def psf_match(coadded, psf_kernel):
    radius = KW // 2
    columns = coadded.shape[2]
    padded = jnp.pad(coadded, ((0, 0), (0, 0), (radius, radius)))
    total = None
    for dy in range(KW):
        for dx in range(KW):
            tap = psf_kernel[:, dy * KW + dx][None, :, None]
            term = tap * padded[dy : dy + TROWS, :, dx : dx + columns].astype(F32)
            total = term if total is None else total + term
    return total.astype(BF16)


def body(
    exposure_pixels,
    block_band,
    block_tile,
    block_row,
    band_weights,
    psf_kernel,
    gal_tile,
    gal_row,
    gal_col,
    gal_shift,
):
    tile_count = lax.axis_size("tile")
    channels, columns = band_weights.shape[1], exposure_pixels.shape[2]
    gal_here = gal_tile.shape[0]
    depth = min(8, gal_here)
    span = 64
    tile_range = jnp.arange(tile_count, dtype=jnp.int32)
    row_range = jnp.arange(TROWS, dtype=jnp.int32)

    strip_range = jnp.arange(tile_count * TROWS, dtype=jnp.int32)
    target = block_tile * TROWS + block_row
    counts_out = jnp.sum((target[None, :] == strip_range[:, None]).astype(jnp.int32), axis=1)
    place = gal_tile * depth + rank_before(gal_tile)
    word = (gal_row * columns + gal_col) * span + gal_shift
    slot_range = jnp.arange(tile_count * depth, dtype=jnp.int32)
    words_out = jnp.sum(
        jnp.where(place[None, :] == slot_range[:, None], word[None, :], 0), axis=1
    )
    mine = (place[:, None] == slot_range[None, :]).astype(BF16)
    counts_out = counts_out.reshape(tile_count, TROWS)
    words_out = words_out.reshape(tile_count, depth)
    if tile_count == 16:
        return small_body(
            exposure_pixels, block_band, block_tile, block_row, band_weights, psf_kernel,
            counts_out, words_out, mine,
        )
    coadded, words = averaged_rows_any(
        exposure_pixels, block_band, block_tile, block_row, band_weights, counts_out, words_out
    )
    slot_shift = words % span
    slot_col = (words // span) % columns
    slot_row = words // (span * columns)
    matched_cube = psf_match(coadded, psf_kernel)

    column_range = jnp.arange(columns, dtype=jnp.int32)
    chosen = (
        (slot_row[None, None, :] == row_range[:, None, None])
        & (slot_col[None, None, :] == column_range[None, :, None])
    ).astype(BF16)
    spectra = lax.dot_general(
        matched_cube, chosen, (((0, 2), (0, 1)), ((), ())), preferred_element_type=F32
    )
    window = jnp.arange(NW, dtype=jnp.int32)
    channel_range = jnp.arange(channels, dtype=jnp.int32)
    inside = channel_range[None, :, None] == (slot_shift[None, :] + window[:, None])[:, None, :]
    values = jnp.sum(jnp.where(inside, spectra[None], 0.0), axis=1).T.astype(BF16)
    returned = lax.all_to_all(values, "tile", split_axis=0, concat_axis=0, tiled=True)
    rest_spectra = jnp.dot(mine, returned, preferred_element_type=F32).astype(BF16)
    return matched_cube, rest_spectra


def solution(mesh):
    one = P(("groups", "tile"))
    cube = P(("groups", "tile"), None, None)
    return jax.shard_map(
        body,
        mesh=mesh,
        in_specs=(cube, one, one, one, P(), P(), one, one, one, one),
        out_specs=(cube, P(("groups", "tile"), None)),
        check_vma=False,
    )
```

```python
import jax
import jax.numpy as jnp
from jax import lax
from jax.experimental import pallas as pl
from jax.experimental.pallas import tpu as pltpu
from jax.sharding import PartitionSpec as P

KW = 5
NW = 64
TROWS = 16
F32 = jnp.float32
BF16 = jnp.bfloat16
CHUNKS = 8
PART = TROWS // CHUNKS
SLAB = 4 * PART
ORDER = (0, 7, 1, 2, 3, 4, 5, 6)
MESH = pl.DeviceIdType.MESH
GROUP = 8


def partial_sums_kernel(
    place_ref, band_ref, pixels_hbm, weights_t_ref, keep_hbm, send_hbm,
    total, pixels_ref, weights_ref, keep_ref, send_ref, in_sem, out_sem,
):
    load = pltpu.make_async_copy(pixels_hbm, pixels_ref, in_sem)
    load.start()
    for band in range(weights_ref.shape[0]):
        weights_ref[band] = weights_t_ref[band].astype(F32).T.astype(BF16)
    blocks = pixels_ref.shape[0]
    half = total.shape[0] // 2

    def clear(i, _):
        total[i] = jnp.zeros(total.shape[1:], F32)
        return 0

    lax.fori_loop(0, total.shape[0], clear, 0, unroll=4)
    load.wait()

    def step(i, _):
        spectra = []
        for k in range(GROUP):
            b = i * GROUP + k
            spectra.append(
                jnp.dot(weights_ref[band_ref[b]], pixels_ref[b], preferred_element_type=F32)
            )
        for k in range(GROUP):
            b = i * GROUP + k
            total[place_ref[b]] += spectra[k].astype(BF16).astype(F32)
        return 0

    lax.fori_loop(0, blocks // GROUP, step, 0)

    copies = []
    for far in (1, 0):
        rows = pl.ds(far * half // 2, half // 2)
        for n, (buffer, out) in enumerate(((send_ref, send_hbm), (keep_ref, keep_hbm))):
            source = (half if n == 0 else 0) + far * half // 2

            def emit(i, _, buffer=buffer, source=source, far=far):
                buffer[far * half // 2 + i] = total[source + i].astype(BF16)
                return 0

            lax.fori_loop(0, half // 2, emit, 0, unroll=4)
            copy = pltpu.make_async_copy(buffer.at[rows], out.at[rows], out_sem.at[2 * far + n])
            copy.start()
            copies.append(copy)
    for copy in copies:
        copy.wait()


def partial_sums(place, band, pixels, weights, rows):
    channels, columns = weights.shape[1], pixels.shape[2]
    smem = pl.BlockSpec(memory_space=pltpu.SMEM)
    vmem = pl.BlockSpec(memory_space=pltpu.VMEM)
    return pl.pallas_call(
        partial_sums_kernel,
        out_shape=[jax.ShapeDtypeStruct((rows // 2, channels, columns), BF16)] * 2,
        in_specs=[smem, smem, pl.BlockSpec(memory_space=pl.ANY), vmem],
        out_specs=[pl.BlockSpec(memory_space=pl.ANY)] * 2,
        scratch_shapes=[
            pltpu.VMEM((rows, channels, columns), F32),
            pltpu.VMEM(pixels.shape, BF16),
            pltpu.VMEM(weights.shape, BF16),
            pltpu.VMEM((rows // 2, channels, columns), BF16),
            pltpu.VMEM((rows // 2, channels, columns), BF16),
            pltpu.SemaphoreType.DMA,
            pltpu.SemaphoreType.DMA((4,)),
        ],
        compiler_params=pltpu.CompilerParams(vmem_limit_bytes=28 * 1024 * 1024),
        name="partial_sums",
    )(place, band, pixels, jnp.swapaxes(weights, 1, 2))


def greet_all(me, count):
    barrier = pltpu.get_barrier_semaphore()

    def hello(k, _):
        pl.semaphore_signal(
            barrier, inc=1, device_id={"tile": (me + k) % count}, device_id_type=MESH
        )
        return 0

    lax.fori_loop(1, count, hello, 0)
    pl.semaphore_wait(barrier, count - 1)


def exchange_copy(k, me, count, out_ref, in_ref, send_sem, recv_sem):
    there = (me + k) % count
    return pltpu.make_async_remote_copy(
        src_ref=out_ref.at[there],
        dst_ref=in_ref.at[me],
        send_sem=send_sem.at[k],
        recv_sem=recv_sem.at[k],
        device_id={"tile": there},
        device_id_type=MESH,
    )


def reduce_kernel(
    notes_ref, keep_hbm, send_ref, psf_ref, mine_ref, cube_ref, rest_ref,
    notes_in, keep_ref, from_core, to_x, from_x, plane, chain_out, chain_in, halo_in, rows_ref,
    taps, picked, window_out, window_in,
    note_send, note_recv, window_send, window_recv, keep_sem, core_send, core_recv, x_send, x_recv,
    chain_send, chain_recv, halo_send, halo_recv,
):
    count = 16
    me = lax.axis_index("tile")
    z, x, c = me // 4, (me // 2) % 2, me % 2
    other_core = me + 1 - 2 * c
    other_x = me + 2 - 4 * x
    part, size = PART, SLAB
    channels, columns = cube_ref.shape[1], cube_ref.shape[2]

    def remote(src, dst, send_sem, recv_sem, there):
        return pltpu.make_async_remote_copy(
            src_ref=src, dst_ref=dst, send_sem=send_sem, recv_sem=recv_sem,
            device_id={"tile": there}, device_id_type=MESH,
        )

    def core_copy(far, k):
        at = far * CHUNKS + k
        rows = pl.ds(at * size, size)
        return remote(
            send_ref.at[rows], from_core.at[rows], core_send.at[at], core_recv.at[at], other_core
        )

    def x_copy(k):
        rows = pl.ds(k * size, size)
        return remote(to_x.at[rows], from_x.at[rows], x_send.at[k], x_recv.at[k], other_x)

    def chain_copy(way, k, dist):
        at = (way * CHUNKS + k) * 3 + dist - 1
        there = (me + 4) % count if way == 0 else (me + 12) % count
        rows = pl.ds(at * part, part)
        return remote(
            chain_out.at[rows], chain_in.at[rows], chain_send.at[at], chain_recv.at[at], there
        )

    def note(k):
        return exchange_copy(k, me, count, notes_ref, notes_in, note_send, note_recv)

    def window(k):
        return exchange_copy(k, me, count, window_out, window_in, window_send, window_recv)

    def keep_copy(far):
        rows = pl.ds(far * CHUNKS * size, CHUNKS * size)
        return pltpu.make_async_copy(keep_hbm.at[rows], keep_ref.at[rows], keep_sem.at[far])

    keep_copy(1).start()
    keep_copy(0).start()
    greet_all(me, count)
    for k in range(3):
        core_copy(1, k).start()

    def send_note(k, _):
        note(k).start()
        return 0


    def cross(k):
        core_copy(1, k).wait_recv()

        def add_x(i, _):
            at = (CHUNKS + k) * size + i
            to_x[k * size + i] = (
                keep_ref[at].astype(F32) + from_core[at].astype(F32)
            ).astype(BF16)
            return 0

        lax.fori_loop(0, size, add_x, 0, unroll=2)
        x_copy(k).start()

    keep_copy(1).wait()
    cross(0)
    core_copy(0, 0).start()
    cross(1)
    core_copy(0, 1).start()
    lax.fori_loop(1, count, send_note, 0)

    def wait_note(k, total):
        note(k).wait_recv()
        return total

    lax.fori_loop(1, count, wait_note, 0)
    notes_in[me] = notes_ref[me]
    keep_copy(0).wait()
    words = notes_in[:, TROWS:, :].reshape(-1, 128)
    slot_shift = words & 63
    slot_col = (words >> 6) & 127
    slot_row = words >> 13
    lane = lax.broadcasted_iota(jnp.int32, words.shape, 1)
    on_column = slot_col == lane
    picked[...] = jnp.zeros(picked.shape, F32)
    psf = psf_ref[...].T
    for tap in range(KW * KW):
        taps[tap] = jnp.broadcast_to(psf[:, tap : tap + 1], (channels, columns))
    counts = jnp.maximum(jnp.sum(notes_in[:, :TROWS, :], axis=0).astype(F32), 1.0)

    def sends(way, dist):
        return z + dist <= 3 if way == 0 else z >= dist

    def receives(way, dist):
        if way == 0:
            return jnp.logical_and(z >= 1, z + dist <= 4)
        return jnp.logical_and(z <= 2, z >= dist - 1)

    def hop(k, dist):
        for way in range(2):

            @pl.when(sends(way, dist))
            def _(way=way):
                to_z = z + dist if way == 0 else z - dist
                at = ((way * CHUNKS + k) * 3 + dist - 1) * part
                source = k * size + to_z * part
                edge = z >= 1 if way == 0 else z <= 2
                if dist == 3:
                    def put(i, _):
                        chain_out[at + i] = plane[source + i]
                        return 0

                    lax.fori_loop(0, part, put, 0)
                else:
                    @pl.when(edge)
                    def _():
                        chain_copy(way, k, dist + 1).wait_recv()

                        def put(i, _):
                            chain_out[at + i] = (
                                plane[source + i].astype(F32)
                                + chain_in[at + part + i].astype(F32)
                            ).astype(BF16)
                            return 0

                        lax.fori_loop(0, part, put, 0)

                    @pl.when(jnp.logical_not(edge))
                    def _():
                        def put(i, _):
                            chain_out[at + i] = plane[source + i]
                            return 0

                        lax.fori_loop(0, part, put, 0)
                chain_copy(way, k, dist).start()

    def finish(k):
        up_at, down_at = k * 3 * part, (CHUNKS + k) * 3 * part

        @pl.when(receives(0, 1))
        def _():
            chain_copy(0, k, 1).wait_recv()

        @pl.when(receives(1, 1))
        def _():
            chain_copy(1, k, 1).wait_recv()

        up_on, down_on = z >= 1, z <= 2
        for i in range(part):
            value = plane[k * size + z * part + i].astype(F32)
            value = value + jnp.where(up_on, chain_in[up_at + i].astype(F32), 0.0)
            value = value + jnp.where(down_on, chain_in[down_at + i].astype(F32), 0.0)
            row = ORDER[k] * part + i
            rows_ref[2 + row] = (value / counts[row : row + 1, :]).astype(BF16)

    def halo_copy(way):
        rows = pl.ds(2, 2) if way == 0 else pl.ds(TROWS, 2)
        there = (me + 15) % count if way == 0 else (me + 1) % count
        return remote(
            rows_ref.at[rows], halo_in.at[pl.ds(2 * way, 2)], halo_send.at[way],
            halo_recv.at[way], there,
        )

    def match_row(y, _):
        radius = KW // 2
        near = [rows_ref[y + dy].astype(F32) for dy in range(KW)]
        at = lax.broadcasted_iota(jnp.int32, (channels, columns), 1)
        total = None
        for dx in range(KW):
            term = taps[dx] * near[0]
            for dy in range(1, KW):
                term = term + taps[dy * KW + dx] * near[dy]
            offset = dx - radius
            if offset != 0:
                term = pltpu.roll(term, (-offset) % columns, 1)
                valid = at < columns - offset if offset > 0 else at >= -offset
                term = jnp.where(valid, term, 0.0)
            total = term if total is None else total + term
        matched = total.astype(BF16)
        cube_ref[y] = matched
        chosen = jnp.where(jnp.logical_and(on_column, slot_row == y), 1.0, 0.0).astype(BF16)
        picked[:, :channels] += lax.dot_general(
            chosen, matched, (((1,), (1,)), ((), ())), preferred_element_type=F32
        )
        return 0

    def take_halo():
        @pl.when(me <= count - 2)
        def _():
            halo_copy(0).wait_recv()
            for i in range(2):
                rows_ref[TROWS + 2 + i] = halo_in[i]

        @pl.when(me >= 1)
        def _():
            halo_copy(1).wait_recv()
            for i in range(2):
                rows_ref[i] = halo_in[2 + i]

    def done(k):
        finish(k)
        if k == 0:
            @pl.when(me >= 1)
            def _():
                halo_copy(0).start()
        if k == 1:
            @pl.when(me <= count - 2)
            def _():
                halo_copy(1).start()
        if k == 4:
            take_halo()
            lax.fori_loop(0, 2, match_row, 0)
        if k >= 3:
            lax.fori_loop(2 * k - 4, 2 * k - 2 if k < CHUNKS - 1 else TROWS, match_row, 0)

    for i in range(2):
        rows_ref[i] = jnp.zeros(rows_ref.shape[1:], BF16)
        rows_ref[TROWS + 2 + i] = jnp.zeros(rows_ref.shape[1:], BF16)

    for t in range(CHUNKS + 3):
        if t < CHUNKS:
            x_copy(t).wait_recv()
            if t + 2 < CHUNKS:
                cross(t + 2)
                core_copy(0, t + 2).start()
            if t + 3 < CHUNKS:
                core_copy(1, t + 3).start()
            core_copy(0, t).wait_recv()

            def add_plane(i, _, t=t):
                at = t * size + i
                plane[at] = (
                    keep_ref[at].astype(F32) + from_core[at].astype(F32) + from_x[at].astype(F32)
                ).astype(BF16)
                return 0

            lax.fori_loop(0, size, add_plane, 0, unroll=2)
            hop(t, 3)
        if 0 <= t - 1 < CHUNKS:
            hop(t - 1, 2)
        if 0 <= t - 2 < CHUNKS:
            hop(t - 2, 1)
        if t >= 3:
            done(t - 3)

    chosen_window = picked[...]
    for bit in range(6):
        moved = pltpu.roll(chosen_window, 128 - 2**bit, 1)
        chosen_window = jnp.where((slot_shift >> bit) & 1 == 1, moved, chosen_window)
    window_out[...] = chosen_window.reshape(window_out.shape)

    def send_window(k, _):
        window(k).start()
        return 0

    def take_window(k, _):
        window(k).wait()
        return 0

    lax.fori_loop(1, count, send_window, 0)
    window_in[me] = window_out[me]

    @pl.when(me >= 1)
    def _():
        halo_copy(0).wait_send()

    @pl.when(me <= count - 2)
    def _():
        halo_copy(1).wait_send()

    def wait_note_sent(k, _):
        note(k).wait_send()
        return 0

    lax.fori_loop(1, count, wait_note_sent, 0)
    for k in range(CHUNKS):
        core_copy(1, k).wait_send()
        core_copy(0, k).wait_send()
        x_copy(k).wait_send()
        for way in range(2):
            for dist in (3, 2, 1):
                @pl.when(sends(way, dist))
                def _(way=way, k=k, dist=dist):
                    chain_copy(way, k, dist).wait_send()
    lax.fori_loop(1, count, take_window, 0)
    landed = window_in[...].reshape(-1, 128).astype(BF16)
    rest = jnp.dot(mine_ref[...], landed, preferred_element_type=F32)
    rest_ref[...] = rest[:, :NW].astype(BF16)


def reduce_and_match(notes, keep, send, psf_kernel, mine):
    tail = keep.shape[1:]
    vmem = pl.BlockSpec(memory_space=pltpu.VMEM)
    hbm = pl.BlockSpec(memory_space=pl.ANY)
    dma = pltpu.SemaphoreType.DMA
    slots = mine.shape[1]
    return pl.pallas_call(
        reduce_kernel,
        out_shape=[
            jax.ShapeDtypeStruct((TROWS,) + tail, BF16),
            jax.ShapeDtypeStruct((mine.shape[0], NW), BF16),
        ],
        in_specs=[vmem, hbm, hbm, vmem, vmem],
        out_specs=[vmem] * 2,
        scratch_shapes=[
            pltpu.VMEM(notes.shape, jnp.int32),
            pltpu.VMEM((8 * TROWS,) + tail, BF16),
            pltpu.VMEM((8 * TROWS,) + tail, BF16),
            pltpu.VMEM((4 * TROWS,) + tail, BF16),
            pltpu.VMEM((4 * TROWS,) + tail, BF16),
            pltpu.VMEM((4 * TROWS,) + tail, BF16),
            pltpu.VMEM((6 * TROWS,) + tail, BF16),
            pltpu.VMEM((6 * TROWS,) + tail, BF16),
            pltpu.VMEM((4,) + tail, BF16),
            pltpu.VMEM((TROWS + 4,) + tail, BF16),
            pltpu.VMEM((KW * KW,) + tail, F32),
            pltpu.VMEM((slots, 128), F32),
            pltpu.VMEM((16, slots // 16, 128), F32),
            pltpu.VMEM((16, slots // 16, 128), F32),
            dma((16,)), dma((16,)), dma((16,)), dma((16,)), dma((2,)),
            dma((2 * CHUNKS,)), dma((2 * CHUNKS,)),
            dma((CHUNKS,)), dma((CHUNKS,)),
            dma((6 * CHUNKS,)), dma((6 * CHUNKS,)),
            dma((2,)), dma((2,)),
        ],
        compiler_params=pltpu.CompilerParams(
            collective_id=0, has_side_effects=True, vmem_limit_bytes=28 * 1024 * 1024
        ),
        name="reduce_and_match",
    )(notes, keep, send, psf_kernel.T, mine)


def small_body(pixels, band, tile, row, weights, psf_kernel, counts_out, words_out, mine):
    me = lax.axis_index("tile")
    x, c = (me // 2) % 2, me % 2
    dest_z, dest_x, dest_c = tile // 4, (tile // 2) % 2, tile % 2
    far_x, far_c = (dest_x + x) % 2, (dest_c + c) % 2
    pair = row // PART
    chunk = jnp.where(pair == 0, 0, jnp.where(pair == CHUNKS - 1, 1, pair + 1))
    place = (((far_c * 2 + far_x) * CHUNKS + chunk) * 4 + dest_z) * PART + row % PART
    keep, send = partial_sums(place, band, pixels, weights, 16 * TROWS)
    notes = jnp.concatenate([counts_out, words_out], axis=1)
    notes = jnp.broadcast_to(notes[:, :, None], notes.shape + (128,))
    return reduce_and_match(notes, keep, send, psf_kernel, mine)


def averaged_rows_any(pixels, band, tile, row, weights, counts_out, words_out):
    sent = jnp.concatenate([counts_out, words_out], axis=1)
    got = lax.all_to_all(sent, "tile", split_axis=0, concat_axis=0, tiled=True)
    counts = jnp.sum(got[:, :TROWS], axis=0).astype(F32)
    row_sums = tile_row_sums_any(pixels, band, tile, row, weights)
    rows = (row_sums / jnp.maximum(counts, 1.0)[:, None, None]).astype(BF16)
    return with_halo(rows, KW // 2), got[:, TROWS:].reshape(-1)


def tile_row_sums_any(pixels, band, tile, row, weights):
    tile_count = lax.axis_size("tile")
    blocks = pixels.shape[0]
    capacity = 2 * blocks // tile_count
    slots = tile_count * capacity
    place = tile * capacity + rank_before(tile)
    tag = jnp.full((slots,), -1, jnp.int32).at[place].set(row * weights.shape[0] + band)
    packed = jnp.zeros((slots,) + pixels.shape[1:], BF16).at[place].set(pixels)
    packed = lax.all_to_all(packed, "tile", split_axis=0, concat_axis=0, tiled=True)
    tag = lax.all_to_all(tag, "tile", split_axis=0, concat_axis=0, tiled=True)
    bands = jnp.maximum(tag, 0) % weights.shape[0]
    rows = jnp.where(tag < 0, -1, tag // weights.shape[0])
    spectra = jnp.einsum("bcs,bsp->bcp", weights[bands], packed, preferred_element_type=F32)
    spectra = spectra.astype(BF16).reshape(slots, -1)
    table = (rows[None, :] == jnp.arange(TROWS)[:, None]).astype(BF16)
    sums = jnp.dot(table, spectra, preferred_element_type=F32)
    return sums.reshape(TROWS, weights.shape[1], pixels.shape[2])


def rank_before(tiles):
    positions = jnp.arange(tiles.shape[0], dtype=jnp.int32)
    earlier = (tiles[:, None] == tiles[None, :]) & (positions[None, :] < positions[:, None])
    return jnp.sum(earlier.astype(jnp.int32), axis=-1)


def with_halo(cells, width):
    count = lax.axis_size("tile")
    ends = count - 1
    above = lax.ppermute(cells[-width:], "tile", [(i, i + 1) for i in range(ends)])
    below = lax.ppermute(cells[:width], "tile", [(i + 1, i) for i in range(ends)])
    return jnp.concatenate([above, cells, below], axis=0)


def psf_match(coadded, psf_kernel):
    radius = KW // 2
    columns = coadded.shape[2]
    padded = jnp.pad(coadded, ((0, 0), (0, 0), (radius, radius)))
    total = None
    for dy in range(KW):
        for dx in range(KW):
            tap = psf_kernel[:, dy * KW + dx][None, :, None]
            term = tap * padded[dy : dy + TROWS, :, dx : dx + columns].astype(F32)
            total = term if total is None else total + term
    return total.astype(BF16)


def body(
    exposure_pixels,
    block_band,
    block_tile,
    block_row,
    band_weights,
    psf_kernel,
    gal_tile,
    gal_row,
    gal_col,
    gal_shift,
):
    tile_count = lax.axis_size("tile")
    channels, columns = band_weights.shape[1], exposure_pixels.shape[2]
    gal_here = gal_tile.shape[0]
    depth = min(8, gal_here)
    span = 64
    tile_range = jnp.arange(tile_count, dtype=jnp.int32)
    row_range = jnp.arange(TROWS, dtype=jnp.int32)

    strip_range = jnp.arange(tile_count * TROWS, dtype=jnp.int32)
    target = block_tile * TROWS + block_row
    counts_out = jnp.sum((target[None, :] == strip_range[:, None]).astype(jnp.int32), axis=1)
    place = gal_tile * depth + rank_before(gal_tile)
    word = (gal_row * columns + gal_col) * span + gal_shift
    slot_range = jnp.arange(tile_count * depth, dtype=jnp.int32)
    words_out = jnp.sum(
        jnp.where(place[None, :] == slot_range[:, None], word[None, :], 0), axis=1
    )
    mine = (place[:, None] == slot_range[None, :]).astype(BF16)
    counts_out = counts_out.reshape(tile_count, TROWS)
    words_out = words_out.reshape(tile_count, depth)
    if tile_count == 16:
        return small_body(
            exposure_pixels, block_band, block_tile, block_row, band_weights, psf_kernel,
            counts_out, words_out, mine,
        )
    coadded, words = averaged_rows_any(
        exposure_pixels, block_band, block_tile, block_row, band_weights, counts_out, words_out
    )
    slot_shift = words % span
    slot_col = (words // span) % columns
    slot_row = words // (span * columns)
    matched_cube = psf_match(coadded, psf_kernel)

    column_range = jnp.arange(columns, dtype=jnp.int32)
    chosen = (
        (slot_row[None, None, :] == row_range[:, None, None])
        & (slot_col[None, None, :] == column_range[None, :, None])
    ).astype(BF16)
    spectra = lax.dot_general(
        matched_cube, chosen, (((0, 2), (0, 1)), ((), ())), preferred_element_type=F32
    )
    window = jnp.arange(NW, dtype=jnp.int32)
    channel_range = jnp.arange(channels, dtype=jnp.int32)
    inside = channel_range[None, :, None] == (slot_shift[None, :] + window[:, None])[:, None, :]
    values = jnp.sum(jnp.where(inside, spectra[None], 0.0), axis=1).T.astype(BF16)
    returned = lax.all_to_all(values, "tile", split_axis=0, concat_axis=0, tiled=True)
    rest_spectra = jnp.dot(mine, returned, preferred_element_type=F32).astype(BF16)
    return matched_cube, rest_spectra


def solution(mesh):
    one = P(("groups", "tile"))
    cube = P(("groups", "tile"), None, None)
    return jax.shard_map(
        body,
        mesh=mesh,
        in_specs=(cube, one, one, one, P(), P(), one, one, one, one),
        out_specs=(cube, P(("groups", "tile"), None)),
        check_vma=False,
    )
```
